32 devices in a mesh: pairs: 2 (over y), pb: 4 (over z), ka: 2 (over core), wa: 2 (over x).
Axes of the slice: x: 2, y: 2, z: 4, core: 2. Of those that a mesh axis runs over, the one named last changes fastest.
Arguments:
- clean_rows: bfloat16 [4096, 8192], P(('pairs', 'pb', 'ka'), 'wa'), parts along dimension 0, may hold values from -72 to 72
- noised_rows: bfloat16 [4096, 8192], P(('pairs', 'pb', 'ka'), 'wa'), parts along dimension 0, may hold values from -6 to 6
- query_weight: bfloat16 [8192, 512], P('wa'), may hold values from -0.0625 to 0.0625
- key_weight: bfloat16 [8192, 128], P('wa'), may hold values from -0.0625 to 0.0625
- value_weight: bfloat16 [8192, 128], P('wa'), may hold values from -0.0625 to 0.0625
- out_grads: bfloat16 [4096, 512], P(('pairs', 'pb', 'ka'), 'wa'), parts along dimension 0, may hold values from -6 to 6
- lookback: int32 [4096], P('pairs'), parts along dimension 0, may hold values from 1 to 2048
Outputs:
- attribution: float32 [4096], P(('pairs', 'pb', 'ka', 'wa')), parts along dimension 0
The draws below stay inside these ranges and needn't reach their ends.
There are 2 independent parts, one for each index of `pairs`. The reference program is written for one: setup_inputs(seed, part) draws one part's arguments, and reference() takes and returns one part's arrays. A program takes and returns all parts, laid end to end along the dimension named above; an argument that names none is the same for every part. Nothing has to cross between parts.
All inputs are finite; a program needn't handle non-finite values.
Results may differ from the reference program's by a relative error of at most 0.01315.
The reference program's roundings to bfloat16 on the way (of `queries`, `keys`, `values` and `noised_keys`) count: a program that leaves them out, or rounds other values in their place, can miss the bound.
Values may be sent and summed in bfloat16 or wider, within the bound.
A program may use at most 64 MiB of HBM per device.

```python
import math
import jax
import jax.numpy as jnp
from jax import lax

D = 8192
HD = 128
H = 4
TOKENS = 2048


def draw_clean_rows(key, part):
    base_key = jax.random.fold_in(jax.random.fold_in(key, 7), 0)
    rows = jax.random.truncated_normal(base_key, -6.0, 6.0, (TOKENS, D), jnp.float32)
    return rows.astype(jnp.bfloat16)


def with_ends(result, key, smallest, high):
    extent = result.shape
    place = [jax.random.randint(jax.random.fold_in(key, axis), (), 0, extent[axis]) for axis in range(len(extent))]
    result = result.at[tuple(place)].set(smallest)
    longest = extent.index(max(extent))
    place[longest] = (place[longest] + 1) % extent[longest]
    return result.at[tuple(place)].set(high)


def level_of(key, dims, cuts, least, high):
    def one(dim, shards_of):
        draws = jax.random.uniform(jax.random.fold_in(jax.random.fold_in(key, 6), dim), (shards_of,), jnp.float32, least / len(cuts), high / len(cuts))
        return jnp.repeat(jnp.exp(draws), dims[dim] // shards_of).reshape((-1,) + (1,) * (len(dims) - dim - 1))

    loudness = one(*cuts[0])
    for cut in cuts[1:]:
        loudness = loudness * one(*cut)
    return loudness


def noise(stream_key, shape, deviation, reach, cuts=(), held_as=jnp.bfloat16):
    array = deviation * jax.random.normal(stream_key, shape, jnp.float32)
    if cuts:
        array = array * level_of(stream_key, shape, cuts, -0.22, 0.18)
    return jnp.clip(array, -reach, reach).astype(held_as)


def setup_inputs(seed: int = 0, part: int = 0) -> dict:
    arg_keys = jax.random.split(jax.random.key(seed), 8)
    part_splits = jax.random.split(jax.random.fold_in(arg_keys[7], part), 8)
    clean_rows = draw_clean_rows(jax.random.fold_in(jax.random.fold_in(arg_keys[7], part), 71), part)
    noised_rows = noise(part_splits[1], (TOKENS, D), 1.0, 6.0, ((0, 8), (1, 2)))
    query_weight = noise(arg_keys[2], (D, H * HD), D ** -0.5, 0.0625, ((0, 2),))
    key_weight = noise(arg_keys[3], (D, HD), D ** -0.5, 0.0625, ((0, 2),))
    value_weight = noise(arg_keys[4], (D, HD), D ** -0.5, 0.0625, ((0, 2),))
    out_grads = noise(part_splits[5], (TOKENS, H * HD), 1.0, 6.0, ((0, 8), (1, 2)))
    lookback = with_ends(jax.random.randint(part_splits[6], (TOKENS,), 1, TOKENS + 1), jax.random.fold_in(part_splits[6], 1), 1, TOKENS).astype(jnp.int32)
    return {"clean_rows": clean_rows, "noised_rows": noised_rows, "query_weight": query_weight, "key_weight": key_weight, "value_weight": value_weight, "out_grads": out_grads, "lookback": lookback}


very_low = -1e+30

def visible_pairs(query_pos, query_look, key_pos):
    distance = query_pos[:, None] - key_pos[None, :]
    return (distance >= 0) & (distance < query_look[:, None])

def block_changes(query_block, grad_block, visible, row_parts, key_block, value_block, noised_block, score_scale):
    highest, row_total, weighted, mean_now = row_parts
    scores = jnp.einsum('bhd,kd->bhk', query_block, key_block, precision=lax.Precision.HIGHEST) * score_scale
    patched = jnp.einsum('bhd,kd->bhk', query_block, noised_block, precision=lax.Precision.HIGHEST) * score_scale
    grad_value = jnp.einsum('bhd,kd->bhk', grad_block, value_block, precision=lax.Precision.HIGHEST)
    held = highest[:, :, None]
    scores = jnp.where(visible, scores, held)
    patched = jnp.where(visible, patched, held)
    shifted = jnp.maximum(held, patched)
    factor = jnp.exp(held - shifted)
    swapped = jnp.exp(patched - shifted) - jnp.exp(scores - shifted)
    divisor = jnp.maximum(row_total[:, :, None] * factor + swapped, 1.0)
    change = (weighted[:, :, None] * factor + swapped * grad_value) / divisor - mean_now[:, :, None]
    return lax.optimization_barrier(jnp.sum(jnp.where(visible, change, 0.0), axis=(0, 1)))

def reference(clean_rows, noised_rows, query_weight, key_weight, value_weight, out_grads, lookback):
    score_scale = 1.0 / math.sqrt(HD)
    queries = jnp.dot(clean_rows, query_weight, preferred_element_type=jnp.float32).astype(jnp.bfloat16)
    keys = jnp.dot(clean_rows, key_weight, preferred_element_type=jnp.float32).astype(jnp.bfloat16)
    values = jnp.dot(clean_rows, value_weight, preferred_element_type=jnp.float32).astype(jnp.bfloat16)
    noised_keys = jnp.dot(noised_rows, key_weight, preferred_element_type=jnp.float32).astype(jnp.bfloat16)
    query_full = queries.astype(jnp.float32).reshape(TOKENS, H, HD)
    grad_full = out_grads.astype(jnp.float32).reshape(TOKENS, H, HD)
    key_full = keys.astype(jnp.float32)
    value_full = values.astype(jnp.float32)
    noised_full = noised_keys.astype(jnp.float32)
    positions = jnp.arange(TOKENS, dtype=jnp.int32)
    block_rows = min(512, TOKENS)
    attribution = jnp.zeros((TOKENS,), jnp.float32)
    for block_index in range(TOKENS // block_rows):
        first_row = block_index * block_rows
        end_row = first_row + block_rows
        query_block = query_full[first_row:end_row]
        grad_block = grad_full[first_row:end_row]
        visible = visible_pairs(positions[first_row:end_row], lookback[first_row:end_row], positions[:end_row])[:, None, :]
        scores = jnp.einsum('bhd,kd->bhk', query_block, key_full[:end_row], precision=lax.Precision.HIGHEST) * score_scale
        grad_value = jnp.einsum('bhd,kd->bhk', grad_block, value_full[:end_row], precision=lax.Precision.HIGHEST)
        masked = jnp.where(visible, scores, very_low)
        highest = lax.optimization_barrier(jnp.max(masked, axis=2))
        weights = jnp.where(visible, jnp.exp(masked - highest[:, :, None]), 0.0)
        row_total = lax.optimization_barrier(jnp.sum(weights, axis=2))
        weighted = lax.optimization_barrier(jnp.sum(weights * grad_value, axis=2))
        mean_now = weighted / row_total
        changes = block_changes(query_block, grad_block, visible, (highest, row_total, weighted, mean_now), key_full[:end_row], value_full[:end_row], noised_full[:end_row], score_scale)
        attribution = attribution.at[:end_row].add(changes)
    return attribution
```

```python
import functools
import math

import jax
import jax.numpy as jnp
from jax import lax
from jax.experimental import pallas as pl
from jax.experimental.pallas import tpu as pltpu
from jax.sharding import PartitionSpec as P

very_low = -1e30
keep_limit = 24 * 2**20
vmem_limit = 56 * 2**20
MESH = pl.DeviceIdType.MESH


def dot(left, right):
    return jnp.dot(left, right, preferred_element_type=jnp.float32)


def dot_t(left, right):
    return lax.dot_general(
        left, right, (((1,), (1,)), ((), ())), preferred_element_type=jnp.float32
    )


def kernel(
    sizes,
    clean_hbm,
    noised_hbm,
    wq_hbm,
    wk_hbm,
    wv_hbm,
    grad_hbm,
    look_ref,
    out_ref,
    clean,
    noised,
    wq,
    wkv,
    grad,
    kv_part,
    nk_part,
    q_part,
    kv_in,
    nk_in,
    q_in,
    side,
    qs,
    gs,
    kept,
    top,
    total,
    weighted,
    mean,
    lane_sum,
    att,
    att_in,
    load_sem,
    kv_send,
    kv_recv,
    nk_send,
    nk_recv,
    q_send,
    q_recv,
    ag_send,
    ag_recv,
    z_send,
    z_recv,
    sib_send,
    sib_recv,
    att_send,
    att_recv,
):
    pb, ka, wa, rows, hd, heads, keep = sizes
    piece = rows // wa
    head_cols = heads * hd
    lanes = heads * rows
    scale = math.log2(math.e) / math.sqrt(hd)
    members = pb * ka * wa
    z = lax.axis_index("pb")
    c = lax.axis_index("ka")
    x = lax.axis_index("wa")
    me = (z * ka + c) * wa + x

    def peer(o):
        return lax.rem(x + o, wa)

    loads = [
        pltpu.make_async_copy(clean_hbm, clean, load_sem.at[0]),
        pltpu.make_async_copy(wk_hbm, wkv.at[:, pl.ds(0, hd)], load_sem.at[1]),
        pltpu.make_async_copy(wv_hbm, wkv.at[:, pl.ds(hd, hd)], load_sem.at[2]),
        pltpu.make_async_copy(noised_hbm, noised, load_sem.at[3]),
    ]
    orders = list(range(1, wa)) + [0]
    for o in orders:
        cols = pl.ds(pl.multiple_of(peer(o) * head_cols, 128), head_cols)
        loads.append(pltpu.make_async_copy(wq_hbm.at[:, cols], wq.at[o], load_sem.at[5 + o]))
    loads.append(pltpu.make_async_copy(grad_hbm, grad, load_sem.at[4]))
    for load in loads:
        load.start()

    barrier = pltpu.get_barrier_semaphore()

    def place(t):
        return {"pb": t // (ka * wa), "ka": (t // wa) % ka, "wa": t % wa}

    def greet(t, carry):
        @pl.when(t != me)
        def _():
            pl.semaphore_signal(barrier, inc=1, device_id=place(t), device_id_type=MESH)

        return carry

    lax.fori_loop(0, members, greet, 0)

    def remote(src, dst, send, recv, where):
        return pltpu.make_async_remote_copy(
            src_ref=src,
            dst_ref=dst,
            send_sem=send,
            recv_sem=recv,
            device_id=where,
            device_id_type=MESH,
        )

    def part_rows(p):
        return pl.ds(pl.multiple_of(p * piece, piece), piece)

    for load in loads[:3]:
        load.wait()
    kv_part[...] = dot(clean[...], wkv[...])
    pl.semaphore_wait(barrier, members - 1)
    kv_copies = []
    for o in range(1, wa):
        p = peer(o)
        copy = remote(
            kv_part.at[part_rows(p)], kv_in.at[wa - o], kv_send.at[o], kv_recv.at[wa - o], {"wa": p}
        )
        copy.start()
        kv_copies.append(copy)
    loads[3].wait()
    nk_part[...] = dot(noised[...], wkv[:, :hd])
    nk_copies = []
    for o in range(1, wa):
        p = peer(o)
        copy = remote(
            nk_part.at[part_rows(p)], nk_in.at[wa - o], nk_send.at[o], nk_recv.at[wa - o], {"wa": p}
        )
        copy.start()
        nk_copies.append(copy)
    q_copies = []
    for n, o in enumerate(orders):
        loads[4 + n].wait()
        q_part[o] = dot(clean[...], wq[o])
        if o:
            copy = remote(
                q_part.at[o], q_in.at[wa - o], q_send.at[o], q_recv.at[wa - o], {"wa": peer(o)}
            )
            copy.start()
            q_copies.append(copy)

    mine = part_rows(x)
    for copy in kv_copies:
        copy.wait_recv()
    kv_sum = kv_part[mine, :]
    for o in range(1, wa):
        kv_sum = kv_sum + kv_in[o]
    side[z, c, mine, pl.ds(0, 2 * hd)] = kv_sum.astype(jnp.bfloat16)
    for copy in nk_copies:
        copy.wait_recv()
    nk_sum = nk_part[mine, :]
    for o in range(1, wa):
        nk_sum = nk_sum + nk_in[o]
    side[z, c, mine, pl.ds(2 * hd, hd)] = nk_sum.astype(jnp.bfloat16)
    ag_copies = []
    for o in range(1, wa):
        own = side.at[z, c, mine]
        copy = remote(own, own, ag_send.at[o], ag_recv.at[wa - o], {"wa": peer(o)})
        copy.start()
        ag_copies.append(copy)
    for o in range(1, wa):
        theirs = side.at[z, c, part_rows(peer(wa - o))]
        remote(theirs, theirs, ag_send.at[o], ag_recv.at[wa - o], {"wa": peer(o)}).wait_recv()

    def up(zz):
        block = side.at[zz, c]
        return remote(block, block, z_send.at[zz], z_recv.at[zz], {"pb": z + 1})

    def across(zz, o):
        block = side.at[zz, c]
        return remote(
            block, block, sib_send.at[zz, o], sib_recv.at[zz, ka - o], {"ka": lax.rem(c + o, ka)}
        )

    def pass_on(zz):
        @pl.when(z + 1 < pb)
        def _():
            up(zz).start()

        for o in range(1, ka):

            @pl.when((zz < z) | (c + o < ka))
            def _():
                across(zz, o).start()

    def arrive(zz):
        block = side.at[zz, c]
        remote(block, block, z_send.at[zz], z_recv.at[zz], {"pb": z - 1}).wait_recv()
        pass_on(zz)

    pass_on(z)

    @pl.when(z >= 1)
    def _():
        arrive(z - 1)

    loads[-1].wait()
    for copy in q_copies:
        copy.wait_recv()
    q_sum = q_part[0]
    for o in range(1, wa):
        q_sum = q_sum + q_in[o]
    q_sum = q_sum.astype(jnp.bfloat16)
    for h in range(heads):
        qs[pl.ds(h * rows, rows), :] = q_sum[:, h * hd : (h + 1) * hd]
        gs[pl.ds(h * rows, rows), :] = grad[:, h * hd : (h + 1) * hd]

    group_rows = rows // 128
    first_look = (z * ka + c) * group_rows
    look = jnp.concatenate(
        [look_ref[pl.ds(first_look + i, 1), :] for i in range(group_rows)] * heads, axis=1
    )
    last_key = (z * ka + c) * rows + jnp.concatenate(
        [lax.broadcasted_iota(jnp.int32, (1, rows), 1)] * heads, axis=1
    )
    before_key = last_key - look

    def products(zz, cc):
        key_pos = (zz * ka + cc) * rows + lax.broadcasted_iota(jnp.int32, (rows, lanes), 0)
        visible = (key_pos <= last_key) & (key_pos > before_key)
        scores = dot_t(side[zz, cc, :, pl.ds(0, hd)], qs[...]) * scale
        patched = dot_t(side[zz, cc, :, pl.ds(2 * hd, hd)], qs[...]) * scale
        grad_value = dot_t(side[zz, cc, :, pl.ds(hd, hd)], gs[...])
        return (
            jnp.where(visible, scores, very_low),
            jnp.where(visible, patched, very_low),
            grad_value,
        )

    top[...] = jnp.full((1, lanes), very_low, jnp.float32)
    total[...] = jnp.zeros((1, lanes), jnp.float32)
    weighted[...] = jnp.zeros((1, lanes), jnp.float32)

    def stats(zz, cc):
        scores, patched, grad_value = products(zz, cc)
        if keep:
            kept[zz, cc, 0] = scores
            kept[zz, cc, 1] = patched
            kept[zz, cc, 2] = grad_value
        highest = jnp.maximum(top[...], jnp.max(scores, axis=0, keepdims=True))
        rescale = jnp.exp2(top[...] - highest)
        weights = jnp.exp2(scores - highest)
        total[...] = total[...] * rescale + jnp.sum(weights, axis=0, keepdims=True)
        weighted[...] = weighted[...] * rescale + jnp.sum(
            weights * grad_value, axis=0, keepdims=True
        )
        top[...] = highest

    def other_stats(zz, o):
        cc = lax.rem(c + ka - o, ka)
        block = side.at[zz, cc]
        remote(block, block, sib_send.at[zz, o], sib_recv.at[zz, ka - o], {"ka": cc}).wait_recv()
        stats(zz, cc)

    stats(z, c)
    for o in range(1, ka):

        @pl.when(c >= o)
        def _():
            other_stats(z, o)

    def earlier(s, carry):
        @pl.when(s <= z)
        def _():
            @pl.when(s >= 2)
            def _():
                arrive(z - s)

            stats(z - s, c)
            for o in range(1, ka):
                other_stats(z - s, o)

        return carry

    lax.fori_loop(1, pb, earlier, 0)

    mean[...] = weighted[...] / jnp.maximum(total[...], 1.0)

    step = 64

    def att_copy(t):
        return remote(att.at[t], att_in.at[me], att_send.at[t], att_recv.at[me], place(t))

    def changes(b, carry):
        zz, cc = b // ka, b % ka

        @pl.when(b <= z * ka + c)
        def _():
            if not keep:
                scores, patched, grad_value = products(zz, cc)
                kept[0, 0, 0] = scores
                kept[0, 0, 1] = patched
                kept[0, 0, 2] = grad_value
            kz, kc = (zz, cc) if keep else (0, 0)

            def chunk(k, carry):
                keys = pl.ds(pl.multiple_of(k * step, step), step)
                so_far = jnp.zeros((step, 128), jnp.float32)
                for q in range(lanes // 128):
                    cols = pl.ds(q * 128, 128)
                    high = top[:, cols]
                    sums = weighted[:, cols]
                    away = kept[kz, kc, 1, keys, cols] - high
                    small = jnp.exp2(-jnp.abs(away))
                    above = away > 0.0
                    factor = jnp.where(above, small, 1.0)
                    swapped = (
                        jnp.where(above, 1.0, small)
                        - jnp.exp2(kept[kz, kc, 0, keys, cols] - high) * factor
                    )
                    divisor = jnp.maximum(total[:, cols] * factor + swapped, 1.0)
                    so_far = so_far + (
                        (sums * factor + swapped * kept[kz, kc, 2, keys, cols]) / divisor
                        - mean[:, cols]
                    )
                lane_sum[keys, :] = so_far
                return carry

            lax.fori_loop(0, rows // step, chunk, 0)
            row = jnp.sum(jnp.transpose(lane_sum[...]), axis=0, keepdims=True)
            for p in range(wa):
                att[b * wa + p] = row[:, p * piece : (p + 1) * piece]

                @pl.when(b * wa + p != me)
                def _():
                    att_copy(b * wa + p).start()

        return carry

    lax.fori_loop(0, pb * ka, changes, 0)

    out_ref[...] = att[me]

    def collect(t, carry):
        @pl.when((t != me) & (t // wa >= z * ka + c))
        def _():
            remote(
                att.at[t], att_in.at[t], att_send.at[t], att_recv.at[t], place(t)
            ).wait_recv()
            out_ref[...] += att_in[t]

        return carry

    lax.fori_loop(0, members, collect, 0)

    for copy in kv_copies + nk_copies + q_copies + ag_copies:
        copy.wait_send()

    def drain(zz, carry):
        @pl.when(zz <= z)
        def _():
            @pl.when(z + 1 < pb)
            def _():
                up(zz).wait_send()

            for o in range(1, ka):

                @pl.when((zz < z) | (c + o < ka))
                def _():
                    across(zz, o).wait_send()

        return carry

    lax.fori_loop(0, pb, drain, 0)

    def drain_att(t, carry):
        @pl.when((t != me) & (t // wa <= z * ka + c))
        def _():
            att_copy(t).wait_send()

        return carry

    lax.fori_loop(0, members, drain_att, 0)


def shards(clean_rows, noised_rows, query_weight, key_weight, value_weight, out_grads, lookback):
    pb, ka, wa = lax.axis_size("pb"), lax.axis_size("ka"), lax.axis_size("wa")
    rows, depth = clean_rows.shape
    hd = key_weight.shape[1]
    head_cols = out_grads.shape[1]
    heads = head_cols // hd
    lanes = heads * rows
    piece = rows // wa
    members = pb * ka * wa
    block = 3 * rows * lanes * 4
    keep = pb * ka * block <= keep_limit
    kept_shape = (pb, ka, 3, rows, lanes) if keep else (1, 1, 3, rows, lanes)
    sizes = (pb, ka, wa, rows, hd, heads, keep)
    bf16, f32 = jnp.bfloat16, jnp.float32
    vmem = pltpu.VMEM
    sem = pltpu.SemaphoreType.DMA
    out = pl.pallas_call(
        functools.partial(kernel, sizes),
        out_shape=jax.ShapeDtypeStruct((1, piece), f32),
        in_specs=[pl.BlockSpec(memory_space=pl.ANY)] * 6 + [pl.BlockSpec(memory_space=vmem)],
        out_specs=pl.BlockSpec(memory_space=vmem),
        scratch_shapes=[
            vmem((rows, depth), bf16),
            vmem((rows, depth), bf16),
            vmem((wa, depth, head_cols), bf16),
            vmem((depth, 2 * hd), bf16),
            vmem((rows, head_cols), bf16),
            vmem((rows, 2 * hd), f32),
            vmem((rows, hd), f32),
            vmem((wa, rows, head_cols), f32),
            vmem((wa, piece, 2 * hd), f32),
            vmem((wa, piece, hd), f32),
            vmem((wa, rows, head_cols), f32),
            vmem((pb, ka, rows, 3 * hd), bf16),
            vmem((lanes, hd), bf16),
            vmem((lanes, hd), bf16),
            vmem(kept_shape, f32),
            vmem((1, lanes), f32),
            vmem((1, lanes), f32),
            vmem((1, lanes), f32),
            vmem((1, lanes), f32),
            vmem((rows, 128), f32),
            vmem((members, 1, piece), f32),
            vmem((members, 1, piece), f32),
            sem((5 + wa,)),
            sem((wa,)),
            sem((wa,)),
            sem((wa,)),
            sem((wa,)),
            sem((wa,)),
            sem((wa,)),
            sem((wa,)),
            sem((wa,)),
            sem((pb,)),
            sem((pb,)),
            sem((pb, ka)),
            sem((pb, ka)),
            sem((members,)),
            sem((members,)),
        ],
        compiler_params=pltpu.CompilerParams(
            collective_id=0, has_side_effects=True, vmem_limit_bytes=vmem_limit
        ),
    )(
        clean_rows,
        noised_rows,
        query_weight,
        key_weight,
        value_weight,
        out_grads,
        lookback.reshape(-1, 128),
    )
    return out.reshape(piece)


def solution(mesh):
    in_specs = (
        P(("pairs", "pb", "ka"), "wa"),
        P(("pairs", "pb", "ka"), "wa"),
        P("wa", None),
        P("wa", None),
        P("wa", None),
        P(("pairs", "pb", "ka"), "wa"),
        P("pairs"),
    )
    out_specs = P(("pairs", "pb", "ka", "wa"))
    return jax.shard_map(shards, mesh=mesh, in_specs=in_specs, out_specs=out_specs, check_vma=False)
```

```python
import functools
import math

import jax
import jax.numpy as jnp
from jax import lax
from jax.experimental import pallas as pl
from jax.experimental.pallas import tpu as pltpu
from jax.sharding import PartitionSpec as P

very_low = -1e30
keep_limit = 24 * 2**20
vmem_limit = 56 * 2**20
MESH = pl.DeviceIdType.MESH


def dot(left, right):
    return jnp.dot(left, right, preferred_element_type=jnp.float32)


def dot_t(left, right):
    return lax.dot_general(
        left, right, (((1,), (1,)), ((), ())), preferred_element_type=jnp.float32
    )


def kernel(
    sizes,
    clean_hbm,
    noised_hbm,
    wq_hbm,
    wk_hbm,
    wv_hbm,
    grad_hbm,
    look_ref,
    out_ref,
    clean,
    noised,
    wq,
    wkv,
    grad,
    kv_part,
    nk_part,
    q_part,
    kv_in,
    nk_in,
    q_in,
    side,
    qs,
    gs,
    kept,
    top,
    total,
    weighted,
    mean,
    lane_sum,
    att,
    att_in,
    load_sem,
    kv_send,
    kv_recv,
    nk_send,
    nk_recv,
    q_send,
    q_recv,
    ag_send,
    ag_recv,
    z_send,
    z_recv,
    sib_send,
    sib_recv,
    att_send,
    att_recv,
):
    pb, ka, wa, rows, hd, heads, keep = sizes
    piece = rows // wa
    head_cols = heads * hd
    lanes = heads * rows
    scale = math.log2(math.e) / math.sqrt(hd)
    members = pb * ka * wa
    z = lax.axis_index("pb")
    c = lax.axis_index("ka")
    x = lax.axis_index("wa")
    me = (z * ka + c) * wa + x

    def peer(o):
        return lax.rem(x + o, wa)

    half = clean.shape[1] // 2
    loads = []
    for i in range(2):
        part = pl.ds(i * half, half)
        loads += [
            pltpu.make_async_copy(
                clean_hbm.at[:, part], clean.at[:, part], load_sem.at[5 + wa + 3 * i]
            ),
            pltpu.make_async_copy(
                wk_hbm.at[part], wkv.at[part, pl.ds(0, hd)], load_sem.at[6 + wa + 3 * i]
            ),
            pltpu.make_async_copy(
                wv_hbm.at[part], wkv.at[part, pl.ds(hd, hd)], load_sem.at[7 + wa + 3 * i]
            ),
        ]
    loads.append(pltpu.make_async_copy(noised_hbm, noised, load_sem.at[3]))
    orders = list(range(1, wa)) + [0]
    for o in orders:
        cols = pl.ds(pl.multiple_of(peer(o) * head_cols, 128), head_cols)
        loads.append(pltpu.make_async_copy(wq_hbm.at[:, cols], wq.at[o], load_sem.at[5 + o]))
    loads.append(pltpu.make_async_copy(grad_hbm, grad, load_sem.at[4]))
    for load in loads:
        load.start()

    barrier = pltpu.get_barrier_semaphore()

    def place(t):
        return {"pb": t // (ka * wa), "ka": (t // wa) % ka, "wa": t % wa}

    def greet(t, carry):
        @pl.when(t != me)
        def _():
            pl.semaphore_signal(barrier, inc=1, device_id=place(t), device_id_type=MESH)

        return carry

    lax.fori_loop(0, members, greet, 0)

    def remote(src, dst, send, recv, where):
        return pltpu.make_async_remote_copy(
            src_ref=src,
            dst_ref=dst,
            send_sem=send,
            recv_sem=recv,
            device_id=where,
            device_id_type=MESH,
        )

    def part_rows(p):
        return pl.ds(pl.multiple_of(p * piece, piece), piece)

    for load in loads[:3]:
        load.wait()
    kv_part[...] = dot(clean[:, :half], wkv[:half, :])
    for load in loads[3:6]:
        load.wait()
    kv_part[...] += dot(clean[:, half:], wkv[half:, :])
    pl.semaphore_wait(barrier, members - 1)
    kv_copies = []
    for o in range(1, wa):
        p = peer(o)
        copy = remote(
            kv_part.at[part_rows(p)], kv_in.at[wa - o], kv_send.at[o], kv_recv.at[wa - o], {"wa": p}
        )
        copy.start()
        kv_copies.append(copy)
    loads[6].wait()
    nk_part[...] = dot(noised[...], wkv[:, :hd])
    nk_copies = []
    for o in range(1, wa):
        p = peer(o)
        copy = remote(
            nk_part.at[part_rows(p)], nk_in.at[wa - o], nk_send.at[o], nk_recv.at[wa - o], {"wa": p}
        )
        copy.start()
        nk_copies.append(copy)
    q_copies = []
    for n, o in enumerate(orders):
        loads[7 + n].wait()
        q_part[o] = dot(clean[...], wq[o])
        if o:
            copy = remote(
                q_part.at[o], q_in.at[wa - o], q_send.at[o], q_recv.at[wa - o], {"wa": peer(o)}
            )
            copy.start()
            q_copies.append(copy)

    mine = part_rows(x)
    for copy in kv_copies:
        copy.wait_recv()
    kv_sum = kv_part[mine, :]
    for o in range(1, wa):
        kv_sum = kv_sum + kv_in[o]
    side[me, :, pl.ds(0, 2 * hd)] = kv_sum.astype(jnp.bfloat16)
    for copy in nk_copies:
        copy.wait_recv()
    nk_sum = nk_part[mine, :]
    for o in range(1, wa):
        nk_sum = nk_sum + nk_in[o]
    side[me, :, pl.ds(2 * hd, hd)] = nk_sum.astype(jnp.bfloat16)

    def owner(zz, cc, xx):
        return (zz * ka + cc) * wa + xx

    def up(zz):
        block = side.at[owner(zz, c, x)]
        return remote(block, block, z_send.at[zz], z_recv.at[zz], {"pb": z + 1})

    def along(zz, o):
        block = side.at[owner(zz, c, x)]
        return remote(block, block, ag_send.at[zz, o], ag_recv.at[zz, wa - o], {"wa": peer(o)})

    def across(zz, w, o):
        block = side.at[owner(zz, c, peer(wa - w))]
        return remote(
            block,
            block,
            sib_send.at[zz, w, o],
            sib_recv.at[zz, w, ka - o],
            {"ka": lax.rem(c + o, ka)},
        )

    def hand_over(zz, w):
        for o in range(1, ka):

            @pl.when((zz < z) | (c + o < ka))
            def _():
                across(zz, w, o).start()

    def pass_on(zz):
        @pl.when(z + 1 < pb)
        def _():
            up(zz).start()

        for o in range(1, wa):
            along(zz, o).start()
        hand_over(zz, 0)

    def arrive(zz):
        block = side.at[owner(zz, c, x)]
        remote(block, block, z_send.at[zz], z_recv.at[zz], {"pb": z - 1}).wait_recv()
        pass_on(zz)

    pass_on(z)

    @pl.when(z >= 1)
    def _():
        arrive(z - 1)

    loads[-1].wait()
    for copy in q_copies:
        copy.wait_recv()
    q_sum = q_part[0]
    for o in range(1, wa):
        q_sum = q_sum + q_in[o]
    q_sum = q_sum.astype(jnp.bfloat16)
    for h in range(heads):
        qs[pl.ds(h * rows, rows), :] = q_sum[:, h * hd : (h + 1) * hd]
        gs[pl.ds(h * rows, rows), :] = grad[:, h * hd : (h + 1) * hd]

    group_rows = rows // 128
    first_look = (z * ka + c) * group_rows
    look = jnp.concatenate(
        [look_ref[pl.ds(first_look + i, 1), :] for i in range(group_rows)] * heads, axis=1
    )
    last_key = (z * ka + c) * rows + jnp.concatenate(
        [lax.broadcasted_iota(jnp.int32, (1, rows), 1)] * heads, axis=1
    )
    before_key = last_key - look

    def products(t):
        key_pos = t * piece + lax.broadcasted_iota(jnp.int32, (piece, lanes), 0)
        visible = (key_pos <= last_key) & (key_pos > before_key)
        scores = dot_t(side[t, :, pl.ds(0, hd)], qs[...]) * scale
        patched = dot_t(side[t, :, pl.ds(2 * hd, hd)], qs[...]) * scale
        grad_value = dot_t(side[t, :, pl.ds(hd, hd)], gs[...])
        return (
            jnp.where(visible, scores, very_low),
            jnp.where(visible, patched, very_low),
            grad_value,
        )

    top[...] = jnp.full((1, lanes), very_low, jnp.float32)
    total[...] = jnp.zeros((1, lanes), jnp.float32)
    weighted[...] = jnp.zeros((1, lanes), jnp.float32)

    def stats(t):
        scores, patched, grad_value = products(t)
        if keep:
            kept[t, 0] = scores
            kept[t, 1] = patched
            kept[t, 2] = grad_value
        highest = jnp.maximum(top[...], jnp.max(scores, axis=0, keepdims=True))
        rescale = jnp.exp2(top[...] - highest)
        weights = jnp.exp2(scores - highest)
        total[...] = total[...] * rescale + jnp.sum(weights, axis=0, keepdims=True)
        weighted[...] = weighted[...] * rescale + jnp.sum(
            weights * grad_value, axis=0, keepdims=True
        )
        top[...] = highest

    def other_cores(zz, w):
        for o in range(1, ka):

            @pl.when((zz < z) | (c >= o))
            def _():
                cc = lax.rem(c + ka - o, ka)
                t = owner(zz, cc, peer(wa - w))
                block = side.at[t]
                remote(
                    block, block, sib_send.at[zz, w, o], sib_recv.at[zz, w, ka - o], {"ka": cc}
                ).wait_recv()
                stats(t)

    def group(s, carry):
        @pl.when(s <= z)
        def _():
            zz = z - s
            stats(owner(zz, c, x))
            other_cores(zz, 0)

            @pl.when((s >= 1) & (s < z))
            def _():
                arrive(zz - 1)

            for w in range(1, wa):
                t = owner(zz, c, peer(wa - w))
                block = side.at[t]
                remote(
                    block, block, ag_send.at[zz, w], ag_recv.at[zz, wa - w], {"wa": peer(w)}
                ).wait_recv()
                hand_over(zz, w)
                stats(t)
                other_cores(zz, w)

        return carry

    lax.fori_loop(0, pb, group, 0)

    mean[...] = weighted[...] * pl.reciprocal(jnp.maximum(total[...], 1.0))

    step = 32

    def att_copy(t):
        return remote(att.at[t], att_in.at[me], att_send.at[t], att_recv.at[me], place(t))

    def changes(t, carry):
        @pl.when(t // wa <= z * ka + c)
        def _():
            if not keep:
                scores, patched, grad_value = products(t)
                kept[0, 0] = scores
                kept[0, 1] = patched
                kept[0, 2] = grad_value
            kt = t if keep else 0

            def chunk(k, carry):
                keys = pl.ds(pl.multiple_of(k * step, step), step)
                so_far = jnp.zeros((step, 128), jnp.float32)
                for q in range(lanes // 128):
                    cols = pl.ds(q * 128, 128)
                    high = top[:, cols]
                    away = kept[kt, 1, keys, cols] - high
                    small = jnp.exp2(-jnp.abs(away))
                    above = away > 0.0
                    factor = jnp.where(above, small, 1.0)
                    swapped = (
                        jnp.where(above, 1.0, small)
                        - jnp.exp2(kept[kt, 0, keys, cols] - high) * factor
                    )
                    divisor = jnp.maximum(total[:, cols] * factor + swapped, 1.0)
                    upper = weighted[:, cols] * factor + swapped * kept[kt, 2, keys, cols]
                    so_far = so_far + (upper * pl.reciprocal(divisor) - mean[:, cols])
                lane_sum[keys, :] = so_far
                return carry

            lax.fori_loop(0, piece // step, chunk, 0)
            att[t] = jnp.sum(jnp.transpose(lane_sum[...]), axis=0, keepdims=True)

            @pl.when(t != me)
            def _():
                att_copy(t).start()

        return carry

    lax.fori_loop(0, members, changes, 0)

    out_ref[...] = att[me]

    def collect(t, carry):
        @pl.when((t != me) & (t // wa >= z * ka + c))
        def _():
            remote(
                att.at[t], att_in.at[t], att_send.at[t], att_recv.at[t], place(t)
            ).wait_recv()
            out_ref[...] += att_in[t]

        return carry

    lax.fori_loop(0, members, collect, 0)

    for copy in kv_copies + nk_copies + q_copies:
        copy.wait_send()

    def drain(zz, carry):
        @pl.when(zz <= z)
        def _():
            @pl.when(z + 1 < pb)
            def _():
                up(zz).wait_send()

            for o in range(1, wa):
                along(zz, o).wait_send()
            for w in range(wa):
                for o in range(1, ka):

                    @pl.when((zz < z) | (c + o < ka))
                    def _():
                        across(zz, w, o).wait_send()

        return carry

    lax.fori_loop(0, pb, drain, 0)

    def drain_att(t, carry):
        @pl.when((t != me) & (t // wa <= z * ka + c))
        def _():
            att_copy(t).wait_send()

        return carry

    lax.fori_loop(0, members, drain_att, 0)


def shards(clean_rows, noised_rows, query_weight, key_weight, value_weight, out_grads, lookback):
    pb, ka, wa = lax.axis_size("pb"), lax.axis_size("ka"), lax.axis_size("wa")
    rows, depth = clean_rows.shape
    hd = key_weight.shape[1]
    head_cols = out_grads.shape[1]
    heads = head_cols // hd
    lanes = heads * rows
    piece = rows // wa
    members = pb * ka * wa
    keep = members * 3 * piece * lanes * 4 <= keep_limit
    kept_shape = (members if keep else 1, 3, piece, lanes)
    sizes = (pb, ka, wa, rows, hd, heads, keep)
    bf16, f32 = jnp.bfloat16, jnp.float32
    vmem = pltpu.VMEM
    sem = pltpu.SemaphoreType.DMA
    out = pl.pallas_call(
        functools.partial(kernel, sizes),
        out_shape=jax.ShapeDtypeStruct((1, piece), f32),
        in_specs=[pl.BlockSpec(memory_space=pl.ANY)] * 6 + [pl.BlockSpec(memory_space=vmem)],
        out_specs=pl.BlockSpec(memory_space=vmem),
        scratch_shapes=[
            vmem((rows, depth), bf16),
            vmem((rows, depth), bf16),
            vmem((wa, depth, head_cols), bf16),
            vmem((depth, 2 * hd), bf16),
            vmem((rows, head_cols), bf16),
            vmem((rows, 2 * hd), f32),
            vmem((rows, hd), f32),
            vmem((wa, rows, head_cols), f32),
            vmem((wa, piece, 2 * hd), f32),
            vmem((wa, piece, hd), f32),
            vmem((wa, rows, head_cols), f32),
            vmem((members, piece, 3 * hd), bf16),
            vmem((lanes, hd), bf16),
            vmem((lanes, hd), bf16),
            vmem(kept_shape, f32),
            vmem((1, lanes), f32),
            vmem((1, lanes), f32),
            vmem((1, lanes), f32),
            vmem((1, lanes), f32),
            vmem((piece, 128), f32),
            vmem((members, 1, piece), f32),
            vmem((members, 1, piece), f32),
            sem((11 + wa,)),
            sem((wa,)),
            sem((wa,)),
            sem((wa,)),
            sem((wa,)),
            sem((wa,)),
            sem((wa,)),
            sem((pb, wa)),
            sem((pb, wa)),
            sem((pb,)),
            sem((pb,)),
            sem((pb, wa, ka)),
            sem((pb, wa, ka)),
            sem((members,)),
            sem((members,)),
        ],
        compiler_params=pltpu.CompilerParams(
            collective_id=0, has_side_effects=True, vmem_limit_bytes=vmem_limit
        ),
    )(
        clean_rows,
        noised_rows,
        query_weight,
        key_weight,
        value_weight,
        out_grads,
        lookback.reshape(-1, 128),
    )
    return out.reshape(piece)


def solution(mesh):
    in_specs = (
        P(("pairs", "pb", "ka"), "wa"),
        P(("pairs", "pb", "ka"), "wa"),
        P("wa", None),
        P("wa", None),
        P("wa", None),
        P(("pairs", "pb", "ka"), "wa"),
        P("pairs"),
    )
    out_specs = P(("pairs", "pb", "ka", "wa"))
    return jax.shard_map(shards, mesh=mesh, in_specs=in_specs, out_specs=out_specs, check_vma=False)
```

```python
import functools
import math

import jax
import jax.numpy as jnp
from jax import lax
from jax.experimental import pallas as pl
from jax.experimental.pallas import tpu as pltpu
from jax.sharding import PartitionSpec as P

very_low = -1e30
keep_limit = 24 * 2**20
vmem_limit = 56 * 2**20
reach = 2
MESH = pl.DeviceIdType.MESH


def dot(left, right):
    return jnp.dot(left, right, preferred_element_type=jnp.float32)


def dot_t(left, right):
    return lax.dot_general(
        left, right, (((1,), (1,)), ((), ())), preferred_element_type=jnp.float32
    )


def kernel(
    sizes,
    clean_hbm,
    noised_hbm,
    wq_hbm,
    wk_hbm,
    wv_hbm,
    grad_hbm,
    look_hbm,
    out_ref,
    clean,
    noised,
    wq,
    wkv,
    grad,
    kv_part,
    nk_part,
    q_part,
    kv_in,
    nk_in,
    q_in,
    side,
    qs,
    gs,
    kept,
    top,
    total,
    weighted,
    mean,
    lane_sum,
    att,
    att_in,
    look_ref,
    load_sem,
    kv_send,
    kv_recv,
    nk_send,
    nk_recv,
    q_send,
    q_recv,
    ag_send,
    ag_recv,
    z_send,
    z_recv,
    next_send,
    next_recv,
    sib_send,
    sib_recv,
    att_send,
    att_recv,
):
    pb, ka, wa, rows, hd, heads, keep = sizes
    piece = rows // wa
    head_cols = heads * hd
    lanes = heads * rows
    scale = math.log2(math.e) / math.sqrt(hd)
    members = pb * ka * wa
    z = lax.axis_index("pb")
    c = lax.axis_index("ka")
    x = lax.axis_index("wa")
    me = (z * ka + c) * wa + x

    def peer(o):
        return lax.rem(x + o, wa)

    half = clean.shape[1] // 2
    loads = []
    for i in range(2):
        part = pl.ds(i * half, half)
        loads += [
            pltpu.make_async_copy(
                clean_hbm.at[:, part], clean.at[:, part], load_sem.at[5 + wa + 3 * i]
            ),
            pltpu.make_async_copy(
                wk_hbm.at[part], wkv.at[part, pl.ds(0, hd)], load_sem.at[6 + wa + 3 * i]
            ),
            pltpu.make_async_copy(
                wv_hbm.at[part], wkv.at[part, pl.ds(hd, hd)], load_sem.at[7 + wa + 3 * i]
            ),
        ]
    loads.append(pltpu.make_async_copy(noised_hbm, noised, load_sem.at[3]))
    orders = list(range(1, wa)) + [0]
    for o in orders:
        cols = pl.ds(pl.multiple_of(peer(o) * head_cols, 128), head_cols)
        loads.append(pltpu.make_async_copy(wq_hbm.at[:, cols], wq.at[o], load_sem.at[5 + o]))
    loads.append(pltpu.make_async_copy(grad_hbm, grad, load_sem.at[4]))
    loads.append(pltpu.make_async_copy(look_hbm, look_ref, load_sem.at[0]))
    for load in loads:
        load.start()

    barrier = pltpu.get_barrier_semaphore()

    def place(t):
        return {"pb": t // (ka * wa), "ka": (t // wa) % ka, "wa": t % wa}

    def greet(t, carry):
        @pl.when(t != me)
        def _():
            pl.semaphore_signal(barrier, inc=1, device_id=place(t), device_id_type=MESH)

        return carry

    lax.fori_loop(0, members, greet, 0)

    def remote(src, dst, send, recv, where):
        return pltpu.make_async_remote_copy(
            src_ref=src,
            dst_ref=dst,
            send_sem=send,
            recv_sem=recv,
            device_id=where,
            device_id_type=MESH,
        )

    def part_rows(p):
        return pl.ds(pl.multiple_of(p * piece, piece), piece)

    for load in loads[:3]:
        load.wait()
    kv_part[...] = dot(clean[:, :half], wkv[:half, :])
    for load in loads[3:6]:
        load.wait()
    kv_part[...] += dot(clean[:, half:], wkv[half:, :])
    pl.semaphore_wait(barrier, members - 1)
    kv_copies = []
    for o in range(1, wa):
        p = peer(o)
        copy = remote(
            kv_part.at[part_rows(p)], kv_in.at[wa - o], kv_send.at[o], kv_recv.at[wa - o], {"wa": p}
        )
        copy.start()
        kv_copies.append(copy)
    loads[6].wait()
    nk_part[...] = dot(noised[...], wkv[:, :hd])
    nk_copies = []
    for o in range(1, wa):
        p = peer(o)
        copy = remote(
            nk_part.at[part_rows(p)], nk_in.at[wa - o], nk_send.at[o], nk_recv.at[wa - o], {"wa": p}
        )
        copy.start()
        nk_copies.append(copy)
    q_copies = []
    for n, o in enumerate(orders):
        loads[7 + n].wait()
        q_part[o] = dot(clean[...], wq[o])
        if o:
            copy = remote(
                q_part.at[o], q_in.at[wa - o], q_send.at[o], q_recv.at[wa - o], {"wa": peer(o)}
            )
            copy.start()
            q_copies.append(copy)

    mine = part_rows(x)
    for copy in kv_copies:
        copy.wait_recv()
    kv_sum = kv_part[mine, :]
    for o in range(1, wa):
        kv_sum = kv_sum + kv_in[o]
    side[me, :, pl.ds(0, 2 * hd)] = kv_sum.astype(jnp.bfloat16)
    for copy in nk_copies:
        copy.wait_recv()
    nk_sum = nk_part[mine, :]
    for o in range(1, wa):
        nk_sum = nk_sum + nk_in[o]
    side[me, :, pl.ds(2 * hd, hd)] = nk_sum.astype(jnp.bfloat16)

    def owner(zz, cc, xx):
        return (zz * ka + cc) * wa + xx

    def up(zz):
        block = side.at[owner(zz, c, x)]
        return remote(block, block, z_send.at[zz], z_recv.at[zz], {"pb": z + 1})

    def along(zz, o):
        block = side.at[owner(zz, c, x)]
        return remote(block, block, ag_send.at[zz, o], ag_recv.at[zz, wa - o], {"wa": peer(o)})

    def across(zz, w, o):
        block = side.at[owner(zz, c, peer(wa - w))]
        return remote(
            block,
            block,
            sib_send.at[zz, w, o],
            sib_recv.at[zz, w, ka - o],
            {"ka": lax.rem(c + o, ka)},
        )

    def next_up(zz, w):
        block = side.at[owner(zz, c, peer(wa - w))]
        return remote(block, block, next_send.at[zz, w], next_recv.at[zz, w], {"pb": z + 1})

    def goes_up(zz):
        return (z + 1 < pb) & (z + 1 - zz <= reach)

    def goes_along(zz):
        return (zz == z) | (z - zz > reach)

    def hand_over(zz, w):
        for o in range(1, ka):

            @pl.when((zz < z) | (c + o < ka))
            def _():
                across(zz, w, o).start()

    def pass_on(zz):
        @pl.when(z + 1 < pb)
        def _():
            up(zz).start()

        @pl.when(goes_along(zz))
        def _():
            for o in range(1, wa):
                along(zz, o).start()

        hand_over(zz, 0)

    def exchanged(zz, w):
        block = side.at[owner(zz, c, peer(wa - w))]

        @pl.when(goes_along(zz))
        def _():
            remote(
                block, block, ag_send.at[zz, w], ag_recv.at[zz, wa - w], {"wa": peer(w)}
            ).wait_recv()

        @pl.when(~goes_along(zz))
        def _():
            remote(
                block, block, next_send.at[zz, w], next_recv.at[zz, w], {"pb": z - 1}
            ).wait_recv()

        @pl.when(goes_up(zz))
        def _():
            next_up(zz, w).start()

        hand_over(zz, w)

    def arrive(zz):
        block = side.at[owner(zz, c, x)]
        remote(block, block, z_send.at[zz], z_recv.at[zz], {"pb": z - 1}).wait_recv()
        pass_on(zz)

    pass_on(z)

    @pl.when(z >= 1)
    def _():
        arrive(z - 1)

    for w in range(1, wa):
        exchanged(z, w)

    loads[-2].wait()
    loads[-1].wait()
    for copy in q_copies:
        copy.wait_recv()
    q_sum = q_part[0]
    for o in range(1, wa):
        q_sum = q_sum + q_in[o]
    q_sum = q_sum.astype(jnp.bfloat16)
    for h in range(heads):
        qs[pl.ds(h * rows, rows), :] = q_sum[:, h * hd : (h + 1) * hd]
        gs[pl.ds(h * rows, rows), :] = grad[:, h * hd : (h + 1) * hd]

    group_rows = rows // 128
    first_look = (z * ka + c) * group_rows
    look = jnp.concatenate(
        [look_ref[pl.ds(first_look + i, 1), :] for i in range(group_rows)] * heads, axis=1
    )
    last_key = (z * ka + c) * rows + jnp.concatenate(
        [lax.broadcasted_iota(jnp.int32, (1, rows), 1)] * heads, axis=1
    )
    before_key = last_key - look

    def products(t):
        key_pos = t * piece + lax.broadcasted_iota(jnp.int32, (piece, lanes), 0)
        visible = (key_pos <= last_key) & (key_pos > before_key)
        scores = dot_t(side[t, :, pl.ds(0, hd)], qs[...]) * scale
        patched = dot_t(side[t, :, pl.ds(2 * hd, hd)], qs[...]) * scale
        grad_value = dot_t(side[t, :, pl.ds(hd, hd)], gs[...])
        return (
            jnp.where(visible, scores, very_low),
            jnp.where(visible, patched, very_low),
            grad_value,
        )

    top[...] = jnp.full((1, lanes), very_low, jnp.float32)
    total[...] = jnp.zeros((1, lanes), jnp.float32)
    weighted[...] = jnp.zeros((1, lanes), jnp.float32)

    def stats(t):
        scores, patched, grad_value = products(t)
        if keep:
            kept[t, 0] = scores
            kept[t, 1] = patched
            kept[t, 2] = grad_value
        highest = jnp.maximum(top[...], jnp.max(scores, axis=0, keepdims=True))
        rescale = jnp.exp2(top[...] - highest)
        weights = jnp.exp2(scores - highest)
        total[...] = total[...] * rescale + jnp.sum(weights, axis=0, keepdims=True)
        weighted[...] = weighted[...] * rescale + jnp.sum(
            weights * grad_value, axis=0, keepdims=True
        )
        top[...] = highest

    def other_cores(zz, w):
        for o in range(1, ka):

            @pl.when((zz < z) | (c >= o))
            def _():
                cc = lax.rem(c + ka - o, ka)
                t = owner(zz, cc, peer(wa - w))
                block = side.at[t]
                remote(
                    block, block, sib_send.at[zz, w, o], sib_recv.at[zz, w, ka - o], {"ka": cc}
                ).wait_recv()
                stats(t)

    def group(s, carry):
        @pl.when(s <= z)
        def _():
            zz = z - s
            stats(owner(zz, c, x))
            other_cores(zz, 0)

            @pl.when((s >= 1) & (s < z))
            def _():
                arrive(zz - 1)

            for w in range(1, wa):

                @pl.when(s >= 1)
                def _():
                    exchanged(zz, w)

                stats(owner(zz, c, peer(wa - w)))
                other_cores(zz, w)

        return carry

    lax.fori_loop(0, pb, group, 0)

    mean[...] = weighted[...] * pl.reciprocal(jnp.maximum(total[...], 1.0))

    step = 32

    def att_copy(t):
        return remote(att.at[t], att_in.at[me], att_send.at[t], att_recv.at[me], place(t))

    def changes(t, carry):
        @pl.when(t // wa <= z * ka + c)
        def _():
            if not keep:
                scores, patched, grad_value = products(t)
                kept[0, 0] = scores
                kept[0, 1] = patched
                kept[0, 2] = grad_value
            kt = t if keep else 0

            def chunk(k, carry):
                keys = pl.ds(pl.multiple_of(k * step, step), step)
                so_far = jnp.zeros((step, 128), jnp.float32)
                for q in range(lanes // 128):
                    cols = pl.ds(q * 128, 128)
                    high = top[:, cols]
                    away = kept[kt, 1, keys, cols] - high
                    small = jnp.exp2(-jnp.abs(away))
                    above = away > 0.0
                    factor = jnp.where(above, small, 1.0)
                    swapped = (
                        jnp.where(above, 1.0, small)
                        - jnp.exp2(kept[kt, 0, keys, cols] - high) * factor
                    )
                    divisor = jnp.maximum(total[:, cols] * factor + swapped, 1.0)
                    upper = weighted[:, cols] * factor + swapped * kept[kt, 2, keys, cols]
                    so_far = so_far + (upper * pl.reciprocal(divisor) - mean[:, cols])
                lane_sum[keys, :] = so_far
                return carry

            lax.fori_loop(0, piece // step, chunk, 0)
            att[t] = jnp.sum(jnp.transpose(lane_sum[...]), axis=0, keepdims=True)

            @pl.when(t != me)
            def _():
                att_copy(t).start()

        return carry

    lax.fori_loop(0, members, changes, 0)

    out_ref[...] = att[me]

    def collect(t, carry):
        @pl.when((t != me) & (t // wa >= z * ka + c))
        def _():
            remote(
                att.at[t], att_in.at[t], att_send.at[t], att_recv.at[t], place(t)
            ).wait_recv()
            out_ref[...] += att_in[t]

        return carry

    lax.fori_loop(0, members, collect, 0)

    for copy in kv_copies + nk_copies + q_copies:
        copy.wait_send()

    def drain(zz, carry):
        @pl.when(zz <= z)
        def _():
            @pl.when(z + 1 < pb)
            def _():
                up(zz).wait_send()

            @pl.when(goes_along(zz))
            def _():
                for o in range(1, wa):
                    along(zz, o).wait_send()

            @pl.when(goes_up(zz))
            def _():
                for w in range(1, wa):
                    next_up(zz, w).wait_send()

            for w in range(wa):
                for o in range(1, ka):

                    @pl.when((zz < z) | (c + o < ka))
                    def _():
                        across(zz, w, o).wait_send()

        return carry

    lax.fori_loop(0, pb, drain, 0)

    def drain_att(t, carry):
        @pl.when((t != me) & (t // wa <= z * ka + c))
        def _():
            att_copy(t).wait_send()

        return carry

    lax.fori_loop(0, members, drain_att, 0)


def shards(clean_rows, noised_rows, query_weight, key_weight, value_weight, out_grads, lookback):
    pb, ka, wa = lax.axis_size("pb"), lax.axis_size("ka"), lax.axis_size("wa")
    rows, depth = clean_rows.shape
    hd = key_weight.shape[1]
    head_cols = out_grads.shape[1]
    heads = head_cols // hd
    lanes = heads * rows
    piece = rows // wa
    members = pb * ka * wa
    keep = members * 3 * piece * lanes * 4 <= keep_limit
    kept_shape = (members if keep else 1, 3, piece, lanes)
    sizes = (pb, ka, wa, rows, hd, heads, keep)
    bf16, f32 = jnp.bfloat16, jnp.float32
    vmem = pltpu.VMEM
    sem = pltpu.SemaphoreType.DMA
    out = pl.pallas_call(
        functools.partial(kernel, sizes),
        out_shape=jax.ShapeDtypeStruct((1, piece), f32),
        in_specs=[pl.BlockSpec(memory_space=pl.ANY)] * 7,
        out_specs=pl.BlockSpec(memory_space=vmem),
        scratch_shapes=[
            vmem((rows, depth), bf16),
            vmem((rows, depth), bf16),
            vmem((wa, depth, head_cols), bf16),
            vmem((depth, 2 * hd), bf16),
            vmem((rows, head_cols), bf16),
            vmem((rows, 2 * hd), f32),
            vmem((rows, hd), f32),
            vmem((wa, rows, head_cols), f32),
            vmem((wa, piece, 2 * hd), f32),
            vmem((wa, piece, hd), f32),
            vmem((wa, rows, head_cols), f32),
            vmem((members, piece, 3 * hd), bf16),
            vmem((lanes, hd), bf16),
            vmem((lanes, hd), bf16),
            vmem(kept_shape, f32),
            vmem((1, lanes), f32),
            vmem((1, lanes), f32),
            vmem((1, lanes), f32),
            vmem((1, lanes), f32),
            vmem((piece, 128), f32),
            vmem((members, 1, piece), f32),
            vmem((members, 1, piece), f32),
            vmem((members * piece // 128, 128), jnp.int32),
            sem((11 + wa,)),
            sem((wa,)),
            sem((wa,)),
            sem((wa,)),
            sem((wa,)),
            sem((wa,)),
            sem((wa,)),
            sem((pb, wa)),
            sem((pb, wa)),
            sem((pb,)),
            sem((pb,)),
            sem((pb, wa)),
            sem((pb, wa)),
            sem((pb, wa, ka)),
            sem((pb, wa, ka)),
            sem((members,)),
            sem((members,)),
        ],
        compiler_params=pltpu.CompilerParams(
            collective_id=0, has_side_effects=True, vmem_limit_bytes=vmem_limit
        ),
    )(
        clean_rows,
        noised_rows,
        query_weight,
        key_weight,
        value_weight,
        out_grads,
        lookback.reshape(-1, 128),
    )
    return out.reshape(piece)


def solution(mesh):
    in_specs = (
        P(("pairs", "pb", "ka"), "wa"),
        P(("pairs", "pb", "ka"), "wa"),
        P("wa", None),
        P("wa", None),
        P("wa", None),
        P(("pairs", "pb", "ka"), "wa"),
        P("pairs"),
    )
    out_specs = P(("pairs", "pb", "ka", "wa"))
    return jax.shard_map(shards, mesh=mesh, in_specs=in_specs, out_specs=out_specs, check_vma=False)
```

```python
import functools
import math

import jax
import jax.numpy as jnp
from jax import lax
from jax.experimental import pallas as pl
from jax.experimental.pallas import tpu as pltpu
from jax.sharding import PartitionSpec as P

very_low = -1e30
keep_limit = 24 * 2**20
vmem_limit = 56 * 2**20
reach = 2
MESH = pl.DeviceIdType.MESH


def dot(left, right):
    return jnp.dot(left, right, preferred_element_type=jnp.float32)


def kernel(
    sizes,
    clean_hbm,
    noised_hbm,
    wq_hbm,
    wk_hbm,
    wv_hbm,
    grad_hbm,
    look_hbm,
    out_ref,
    clean,
    noised,
    wq,
    wkv,
    grad,
    kv_part,
    nk_part,
    q_part,
    kv_in,
    nk_in,
    q_in,
    side,
    qs,
    gs,
    kept,
    top,
    total,
    weighted,
    mean,
    lane_sum,
    att,
    att_in,
    look_ref,
    load_sem,
    kv_send,
    kv_recv,
    nk_send,
    nk_recv,
    q_send,
    q_recv,
    ag_send,
    ag_recv,
    z_send,
    z_recv,
    next_send,
    next_recv,
    sib_send,
    sib_recv,
    att_send,
    att_recv,
):
    pb, ka, wa, rows, hd, heads, keep = sizes
    piece = rows // wa
    head_cols = heads * hd
    lanes = heads * rows
    scale = math.log2(math.e) / math.sqrt(hd)
    members = pb * ka * wa
    z = lax.axis_index("pb")
    c = lax.axis_index("ka")
    x = lax.axis_index("wa")
    me = (z * ka + c) * wa + x

    def peer(o):
        return lax.rem(x + o, wa)

    half = clean.shape[1] // 2
    loads = []
    for i in range(2):
        part = pl.ds(i * half, half)
        loads += [
            pltpu.make_async_copy(
                clean_hbm.at[:, part], clean.at[:, part], load_sem.at[5 + wa + 3 * i]
            ),
            pltpu.make_async_copy(
                wk_hbm.at[part], wkv.at[part, pl.ds(0, hd)], load_sem.at[6 + wa + 3 * i]
            ),
            pltpu.make_async_copy(
                wv_hbm.at[part], wkv.at[part, pl.ds(hd, hd)], load_sem.at[7 + wa + 3 * i]
            ),
        ]
    loads.append(pltpu.make_async_copy(noised_hbm, noised, load_sem.at[3]))
    orders = list(range(1, wa)) + [0]
    for o in orders:
        cols = pl.ds(pl.multiple_of(peer(o) * head_cols, 128), head_cols)
        loads.append(pltpu.make_async_copy(wq_hbm.at[:, cols], wq.at[o], load_sem.at[5 + o]))
    loads.append(pltpu.make_async_copy(grad_hbm, grad, load_sem.at[4]))
    loads.append(pltpu.make_async_copy(look_hbm, look_ref, load_sem.at[0]))
    for load in loads:
        load.start()

    barrier = pltpu.get_barrier_semaphore()

    def place(t):
        return {"pb": t // (ka * wa), "ka": (t // wa) % ka, "wa": t % wa}

    def greet(t, carry):
        @pl.when(t != me)
        def _():
            pl.semaphore_signal(barrier, inc=1, device_id=place(t), device_id_type=MESH)

        return carry

    lax.fori_loop(0, members, greet, 0)

    def remote(src, dst, send, recv, where):
        return pltpu.make_async_remote_copy(
            src_ref=src,
            dst_ref=dst,
            send_sem=send,
            recv_sem=recv,
            device_id=where,
            device_id_type=MESH,
        )

    def part_rows(p):
        return pl.ds(pl.multiple_of(p * piece, piece), piece)

    for load in loads[:3]:
        load.wait()
    kv_part[...] = dot(clean[:, :half], wkv[:half, :])
    for load in loads[3:6]:
        load.wait()
    kv_part[...] += dot(clean[:, half:], wkv[half:, :])
    pl.semaphore_wait(barrier, members - 1)
    kv_copies = []
    for o in range(1, wa):
        p = peer(o)
        copy = remote(
            kv_part.at[part_rows(p)], kv_in.at[wa - o], kv_send.at[o], kv_recv.at[wa - o], {"wa": p}
        )
        copy.start()
        kv_copies.append(copy)
    loads[6].wait()
    nk_part[...] = dot(noised[...], wkv[:, :hd])
    nk_copies = []
    for o in range(1, wa):
        p = peer(o)
        copy = remote(
            nk_part.at[part_rows(p)], nk_in.at[wa - o], nk_send.at[o], nk_recv.at[wa - o], {"wa": p}
        )
        copy.start()
        nk_copies.append(copy)
    q_copies = []
    for n, o in enumerate(orders[:-1]):
        loads[7 + n].wait()
        q_part[o] = dot(clean[...], wq[o])
        copy = remote(
            q_part.at[o], q_in.at[wa - o], q_send.at[o], q_recv.at[wa - o], {"wa": peer(o)}
        )
        copy.start()
        q_copies.append(copy)

    mine = part_rows(x)
    for copy in kv_copies:
        copy.wait_recv()
    kv_sum = kv_part[mine, :]
    for o in range(1, wa):
        kv_sum = kv_sum + kv_in[o]
    side[me, :, pl.ds(0, 2 * hd)] = kv_sum.astype(jnp.bfloat16)
    for copy in nk_copies:
        copy.wait_recv()
    nk_sum = nk_part[mine, :]
    for o in range(1, wa):
        nk_sum = nk_sum + nk_in[o]
    side[me, :, pl.ds(2 * hd, hd)] = nk_sum.astype(jnp.bfloat16)

    def owner(zz, cc, xx):
        return (zz * ka + cc) * wa + xx

    def up(zz):
        block = side.at[owner(zz, c, x)]
        return remote(block, block, z_send.at[zz], z_recv.at[zz], {"pb": z + 1})

    def along(zz, o):
        block = side.at[owner(zz, c, x)]
        return remote(block, block, ag_send.at[zz, o], ag_recv.at[zz, wa - o], {"wa": peer(o)})

    def across(zz, w, o):
        block = side.at[owner(zz, c, peer(wa - w))]
        return remote(
            block,
            block,
            sib_send.at[zz, w, o],
            sib_recv.at[zz, w, ka - o],
            {"ka": lax.rem(c + o, ka)},
        )

    def next_up(zz, w):
        block = side.at[owner(zz, c, peer(wa - w))]
        return remote(block, block, next_send.at[zz, w], next_recv.at[zz, w], {"pb": z + 1})

    def goes_up(zz):
        return (z + 1 < pb) & (z + 1 - zz <= reach)

    def goes_along(zz):
        return (zz == z) | (z - zz > reach)

    def hand_over(zz, w):
        for o in range(1, ka):

            @pl.when((zz < z) | (c + o < ka))
            def _():
                across(zz, w, o).start()

    def pass_on(zz):
        @pl.when(z + 1 < pb)
        def _():
            up(zz).start()

        @pl.when(goes_along(zz))
        def _():
            for o in range(1, wa):
                along(zz, o).start()

        hand_over(zz, 0)

    def exchanged(zz, w):
        block = side.at[owner(zz, c, peer(wa - w))]

        @pl.when(goes_along(zz))
        def _():
            remote(
                block, block, ag_send.at[zz, w], ag_recv.at[zz, wa - w], {"wa": peer(w)}
            ).wait_recv()

        @pl.when(~goes_along(zz))
        def _():
            remote(
                block, block, next_send.at[zz, w], next_recv.at[zz, w], {"pb": z - 1}
            ).wait_recv()

        @pl.when(goes_up(zz))
        def _():
            next_up(zz, w).start()

        hand_over(zz, w)

    def arrive(zz):
        block = side.at[owner(zz, c, x)]
        remote(block, block, z_send.at[zz], z_recv.at[zz], {"pb": z - 1}).wait_recv()
        pass_on(zz)

    pass_on(z)
    loads[6 + wa].wait()
    q_part[0] = dot(clean[...], wq[0])

    @pl.when(z >= 1)
    def _():
        arrive(z - 1)

    for w in range(1, wa):
        exchanged(z, w)

    loads[-2].wait()
    loads[-1].wait()
    for copy in q_copies:
        copy.wait_recv()
    q_sum = q_part[0]
    for o in range(1, wa):
        q_sum = q_sum + q_in[o]
    q_sum = q_sum.astype(jnp.bfloat16)
    for h in range(heads):
        qs[:, pl.ds(h * rows, rows)] = jnp.transpose(q_sum[:, h * hd : (h + 1) * hd])
        gs[:, pl.ds(h * rows, rows)] = jnp.transpose(grad[:, h * hd : (h + 1) * hd])

    group_rows = rows // 128
    first_look = (z * ka + c) * group_rows
    look = jnp.concatenate(
        [look_ref[pl.ds(first_look + i, 1), :] for i in range(group_rows)] * heads, axis=1
    )
    last_key = (z * ka + c) * rows + jnp.concatenate(
        [lax.broadcasted_iota(jnp.int32, (1, rows), 1)] * heads, axis=1
    )
    before_key = last_key - look

    def products(t):
        key_pos = t * piece + lax.broadcasted_iota(jnp.int32, (piece, lanes), 0)
        visible = (key_pos <= last_key) & (key_pos > before_key)
        both = dot(
            jnp.concatenate([side[t, :, pl.ds(0, hd)], side[t, :, pl.ds(2 * hd, hd)]], axis=0),
            qs[...],
        )
        scores = both[:piece] * scale
        patched = both[piece:] * scale
        grad_value = dot(side[t, :, pl.ds(hd, hd)], gs[...])
        return (
            jnp.where(visible, scores, very_low),
            jnp.where(visible, patched, very_low),
            grad_value,
        )

    top[...] = jnp.full((1, lanes), very_low, jnp.float32)
    total[...] = jnp.zeros((1, lanes), jnp.float32)
    weighted[...] = jnp.zeros((1, lanes), jnp.float32)

    def stats(t):
        scores, patched, grad_value = products(t)
        if keep:
            kept[t, 0] = scores
            kept[t, 1] = patched
            kept[t, 2] = grad_value
        highest = jnp.maximum(top[...], jnp.max(scores, axis=0, keepdims=True))
        rescale = jnp.exp2(top[...] - highest)
        weights = jnp.exp2(scores - highest)
        total[...] = total[...] * rescale + jnp.sum(weights, axis=0, keepdims=True)
        weighted[...] = weighted[...] * rescale + jnp.sum(
            weights * grad_value, axis=0, keepdims=True
        )
        top[...] = highest

    def other_cores(zz, w):
        for o in range(1, ka):

            @pl.when((zz < z) | (c >= o))
            def _():
                cc = lax.rem(c + ka - o, ka)
                t = owner(zz, cc, peer(wa - w))
                block = side.at[t]
                remote(
                    block, block, sib_send.at[zz, w, o], sib_recv.at[zz, w, ka - o], {"ka": cc}
                ).wait_recv()
                stats(t)

    def group(s, carry):
        @pl.when(s <= z)
        def _():
            zz = z - s
            stats(owner(zz, c, x))
            other_cores(zz, 0)

            @pl.when((s >= 1) & (s < z))
            def _():
                arrive(zz - 1)

            for w in range(1, wa):

                @pl.when(s >= 1)
                def _():
                    exchanged(zz, w)

                stats(owner(zz, c, peer(wa - w)))
                other_cores(zz, w)

        return carry

    lax.fori_loop(0, pb, group, 0)

    mean[...] = weighted[...] * pl.reciprocal(
        jnp.maximum(total[...], 1.0), full_range=False
    )

    step = 32

    def att_copy(t):
        return remote(att.at[t], att_in.at[me], att_send.at[t], att_recv.at[me], place(t))

    def changes(t, carry):
        @pl.when(t // wa <= z * ka + c)
        def _():
            if not keep:
                scores, patched, grad_value = products(t)
                kept[0, 0] = scores
                kept[0, 1] = patched
                kept[0, 2] = grad_value
            kt = t if keep else 0

            def chunk(k, carry):
                keys = pl.ds(pl.multiple_of(k * step, step), step)
                so_far = jnp.zeros((step, 128), jnp.float32)
                for q in range(lanes // 128):
                    cols = pl.ds(q * 128, 128)
                    high = top[:, cols]
                    away = kept[kt, 1, keys, cols] - high
                    small = jnp.exp2(-jnp.abs(away))
                    above = away > 0.0
                    factor = jnp.where(above, small, 1.0)
                    swapped = (
                        jnp.where(above, 1.0, small)
                        - jnp.exp2(kept[kt, 0, keys, cols] - high) * factor
                    )
                    divisor = jnp.maximum(total[:, cols] * factor + swapped, 1.0)
                    upper = weighted[:, cols] * factor + swapped * kept[kt, 2, keys, cols]
                    so_far = so_far + (upper * pl.reciprocal(divisor, full_range=False) - mean[:, cols])
                lane_sum[keys, :] = so_far
                return carry

            lax.fori_loop(0, piece // step, chunk, 0)
            att[t] = jnp.sum(jnp.transpose(lane_sum[...]), axis=0, keepdims=True)

            @pl.when(t != me)
            def _():
                att_copy(t).start()

        return carry

    lax.fori_loop(0, members, changes, 0)

    out_ref[...] = att[me]

    def collect(t, carry):
        @pl.when((t != me) & (t // wa >= z * ka + c))
        def _():
            remote(
                att.at[t], att_in.at[t], att_send.at[t], att_recv.at[t], place(t)
            ).wait_recv()
            out_ref[...] += att_in[t]

        return carry

    lax.fori_loop(0, members, collect, 0)

    for copy in kv_copies + nk_copies + q_copies:
        copy.wait_send()

    def drain(zz, carry):
        @pl.when(zz <= z)
        def _():
            @pl.when(z + 1 < pb)
            def _():
                up(zz).wait_send()

            @pl.when(goes_along(zz))
            def _():
                for o in range(1, wa):
                    along(zz, o).wait_send()

            @pl.when(goes_up(zz))
            def _():
                for w in range(1, wa):
                    next_up(zz, w).wait_send()

            for w in range(wa):
                for o in range(1, ka):

                    @pl.when((zz < z) | (c + o < ka))
                    def _():
                        across(zz, w, o).wait_send()

        return carry

    lax.fori_loop(0, pb, drain, 0)

    def drain_att(t, carry):
        @pl.when((t != me) & (t // wa <= z * ka + c))
        def _():
            att_copy(t).wait_send()

        return carry

    lax.fori_loop(0, members, drain_att, 0)


def shards(clean_rows, noised_rows, query_weight, key_weight, value_weight, out_grads, lookback):
    pb, ka, wa = lax.axis_size("pb"), lax.axis_size("ka"), lax.axis_size("wa")
    rows, depth = clean_rows.shape
    hd = key_weight.shape[1]
    head_cols = out_grads.shape[1]
    heads = head_cols // hd
    lanes = heads * rows
    piece = rows // wa
    members = pb * ka * wa
    keep = members * 3 * piece * lanes * 4 <= keep_limit
    kept_shape = (members if keep else 1, 3, piece, lanes)
    sizes = (pb, ka, wa, rows, hd, heads, keep)
    bf16, f32 = jnp.bfloat16, jnp.float32
    vmem = pltpu.VMEM
    sem = pltpu.SemaphoreType.DMA
    out = pl.pallas_call(
        functools.partial(kernel, sizes),
        out_shape=jax.ShapeDtypeStruct((1, piece), f32),
        in_specs=[pl.BlockSpec(memory_space=pl.ANY)] * 7,
        out_specs=pl.BlockSpec(memory_space=vmem),
        scratch_shapes=[
            vmem((rows, depth), bf16),
            vmem((rows, depth), bf16),
            vmem((wa, depth, head_cols), bf16),
            vmem((depth, 2 * hd), bf16),
            vmem((rows, head_cols), bf16),
            vmem((rows, 2 * hd), f32),
            vmem((rows, hd), f32),
            vmem((wa, rows, head_cols), f32),
            vmem((wa, piece, 2 * hd), f32),
            vmem((wa, piece, hd), f32),
            vmem((wa, rows, head_cols), f32),
            vmem((members, piece, 3 * hd), bf16),
            vmem((hd, lanes), bf16),
            vmem((hd, lanes), bf16),
            vmem(kept_shape, f32),
            vmem((1, lanes), f32),
            vmem((1, lanes), f32),
            vmem((1, lanes), f32),
            vmem((1, lanes), f32),
            vmem((piece, 128), f32),
            vmem((members, 1, piece), f32),
            vmem((members, 1, piece), f32),
            vmem((members * piece // 128, 128), jnp.int32),
            sem((11 + wa,)),
            sem((wa,)),
            sem((wa,)),
            sem((wa,)),
            sem((wa,)),
            sem((wa,)),
            sem((wa,)),
            sem((pb, wa)),
            sem((pb, wa)),
            sem((pb,)),
            sem((pb,)),
            sem((pb, wa)),
            sem((pb, wa)),
            sem((pb, wa, ka)),
            sem((pb, wa, ka)),
            sem((members,)),
            sem((members,)),
        ],
        compiler_params=pltpu.CompilerParams(
            collective_id=0, has_side_effects=True, vmem_limit_bytes=vmem_limit
        ),
    )(
        clean_rows,
        noised_rows,
        query_weight,
        key_weight,
        value_weight,
        out_grads,
        lookback.reshape(-1, 128),
    )
    return out.reshape(piece)


def solution(mesh):
    in_specs = (
        P(("pairs", "pb", "ka"), "wa"),
        P(("pairs", "pb", "ka"), "wa"),
        P("wa", None),
        P("wa", None),
        P("wa", None),
        P(("pairs", "pb", "ka"), "wa"),
        P("pairs"),
    )
    out_specs = P(("pairs", "pb", "ka", "wa"))
    return jax.shard_map(shards, mesh=mesh, in_specs=in_specs, out_specs=out_specs, check_vma=False)
```

```python
import functools
import math

import jax
import jax.numpy as jnp
from jax import lax
from jax.experimental import pallas as pl
from jax.experimental.pallas import tpu as pltpu
from jax.sharding import PartitionSpec as P

very_low = -1e30
keep_limit = 24 * 2**20
vmem_limit = 56 * 2**20
reach = 2
MESH = pl.DeviceIdType.MESH


def dot(left, right):
    return jnp.dot(left, right, preferred_element_type=jnp.float32)


def kernel(
    sizes,
    clean_hbm,
    noised_hbm,
    wq_hbm,
    wk_hbm,
    wv_hbm,
    grad_hbm,
    look_hbm,
    out_ref,
    clean,
    noised,
    wq,
    wkv,
    grad,
    kv_part,
    nk_part,
    q_part,
    kv_in,
    nk_in,
    q_in,
    side,
    qs,
    gs,
    kept,
    top,
    total,
    weighted,
    mean,
    att,
    att_in,
    look_ref,
    load_sem,
    kv_send,
    kv_recv,
    nk_send,
    nk_recv,
    q_send,
    q_recv,
    ag_send,
    ag_recv,
    z_send,
    z_recv,
    next_send,
    next_recv,
    sib_send,
    sib_recv,
    att_send,
    att_recv,
):
    pb, ka, wa, rows, hd, heads, keep = sizes
    piece = rows // wa
    head_cols = heads * hd
    lanes = heads * rows
    scale = math.log2(math.e) / math.sqrt(hd)
    members = pb * ka * wa
    z = lax.axis_index("pb")
    c = lax.axis_index("ka")
    x = lax.axis_index("wa")
    me = (z * ka + c) * wa + x

    def peer(o):
        return lax.rem(x + o, wa)

    half = clean.shape[1] // 2
    loads = []
    for i in range(2):
        part = pl.ds(i * half, half)
        loads += [
            pltpu.make_async_copy(
                clean_hbm.at[:, part], clean.at[:, part], load_sem.at[5 + wa + 3 * i]
            ),
            pltpu.make_async_copy(
                wk_hbm.at[part], wkv.at[part, pl.ds(0, hd)], load_sem.at[6 + wa + 3 * i]
            ),
            pltpu.make_async_copy(
                wv_hbm.at[part], wkv.at[part, pl.ds(hd, hd)], load_sem.at[7 + wa + 3 * i]
            ),
        ]
    loads.append(pltpu.make_async_copy(noised_hbm, noised, load_sem.at[3]))
    orders = list(range(1, wa)) + [0]
    for o in orders:
        cols = pl.ds(pl.multiple_of(peer(o) * head_cols, 128), head_cols)
        loads.append(pltpu.make_async_copy(wq_hbm.at[:, cols], wq.at[o], load_sem.at[5 + o]))
    loads.append(pltpu.make_async_copy(grad_hbm, grad, load_sem.at[4]))
    loads.append(pltpu.make_async_copy(look_hbm, look_ref, load_sem.at[0]))
    for load in loads:
        load.start()

    barrier = pltpu.get_barrier_semaphore()

    def place(t):
        return {"pb": t // (ka * wa), "ka": (t // wa) % ka, "wa": t % wa}

    def greet(t, carry):
        @pl.when(t != me)
        def _():
            pl.semaphore_signal(barrier, inc=1, device_id=place(t), device_id_type=MESH)

        return carry

    lax.fori_loop(0, members, greet, 0)

    def remote(src, dst, send, recv, where):
        return pltpu.make_async_remote_copy(
            src_ref=src,
            dst_ref=dst,
            send_sem=send,
            recv_sem=recv,
            device_id=where,
            device_id_type=MESH,
        )

    def part_rows(p):
        return pl.ds(pl.multiple_of(p * piece, piece), piece)

    for load in loads[:3]:
        load.wait()
    kv_part[...] = dot(clean[:, :half], wkv[:half, :])
    for load in loads[3:6]:
        load.wait()
    kv_part[...] += dot(clean[:, half:], wkv[half:, :])
    pl.semaphore_wait(barrier, members - 1)
    kv_copies = []
    for o in range(1, wa):
        p = peer(o)
        copy = remote(
            kv_part.at[part_rows(p)], kv_in.at[wa - o], kv_send.at[o], kv_recv.at[wa - o], {"wa": p}
        )
        copy.start()
        kv_copies.append(copy)
    loads[6].wait()
    nk_part[...] = dot(noised[...], wkv[:, :hd])
    nk_copies = []
    for o in range(1, wa):
        p = peer(o)
        copy = remote(
            nk_part.at[part_rows(p)], nk_in.at[wa - o], nk_send.at[o], nk_recv.at[wa - o], {"wa": p}
        )
        copy.start()
        nk_copies.append(copy)
    q_copies = []
    for n, o in enumerate(orders[:-1]):
        loads[7 + n].wait()
        q_part[o] = dot(clean[...], wq[o])
        copy = remote(
            q_part.at[o], q_in.at[wa - o], q_send.at[o], q_recv.at[wa - o], {"wa": peer(o)}
        )
        copy.start()
        q_copies.append(copy)

    mine = part_rows(x)
    for copy in kv_copies:
        copy.wait_recv()
    kv_sum = kv_part[mine, :]
    for o in range(1, wa):
        kv_sum = kv_sum + kv_in[o]
    side[me, :, pl.ds(0, 2 * hd)] = kv_sum.astype(jnp.bfloat16)
    for copy in nk_copies:
        copy.wait_recv()
    nk_sum = nk_part[mine, :]
    for o in range(1, wa):
        nk_sum = nk_sum + nk_in[o]
    side[me, :, pl.ds(2 * hd, hd)] = nk_sum.astype(jnp.bfloat16)

    def owner(zz, cc, xx):
        return (zz * ka + cc) * wa + xx

    def up(zz):
        block = side.at[owner(zz, c, x)]
        return remote(block, block, z_send.at[zz], z_recv.at[zz], {"pb": z + 1})

    def along(zz, o):
        block = side.at[owner(zz, c, x)]
        return remote(block, block, ag_send.at[zz, o], ag_recv.at[zz, wa - o], {"wa": peer(o)})

    def across(zz, w, o):
        block = side.at[owner(zz, c, peer(wa - w))]
        return remote(
            block,
            block,
            sib_send.at[zz, w, o],
            sib_recv.at[zz, w, ka - o],
            {"ka": lax.rem(c + o, ka)},
        )

    def next_up(zz, w):
        block = side.at[owner(zz, c, peer(wa - w))]
        return remote(block, block, next_send.at[zz, w], next_recv.at[zz, w], {"pb": z + 1})

    def goes_up(zz):
        return (z + 1 < pb) & (z + 1 - zz <= reach)

    def goes_along(zz):
        return (zz == z) | (z - zz > reach)

    def hand_over(zz, w):
        for o in range(1, ka):

            @pl.when((zz < z) | (c + o < ka))
            def _():
                across(zz, w, o).start()

    def pass_on(zz):
        @pl.when(z + 1 < pb)
        def _():
            up(zz).start()

        @pl.when(goes_along(zz))
        def _():
            for o in range(1, wa):
                along(zz, o).start()

        hand_over(zz, 0)

    def exchanged(zz, w):
        block = side.at[owner(zz, c, peer(wa - w))]

        @pl.when(goes_along(zz))
        def _():
            remote(
                block, block, ag_send.at[zz, w], ag_recv.at[zz, wa - w], {"wa": peer(w)}
            ).wait_recv()

        @pl.when(~goes_along(zz))
        def _():
            remote(
                block, block, next_send.at[zz, w], next_recv.at[zz, w], {"pb": z - 1}
            ).wait_recv()

        @pl.when(goes_up(zz))
        def _():
            next_up(zz, w).start()

        hand_over(zz, w)

    def arrive(zz):
        block = side.at[owner(zz, c, x)]
        remote(block, block, z_send.at[zz], z_recv.at[zz], {"pb": z - 1}).wait_recv()
        pass_on(zz)

    pass_on(z)
    loads[6 + wa].wait()
    q_part[0] = dot(clean[...], wq[0])

    @pl.when(z >= 1)
    def _():
        arrive(z - 1)

    for w in range(1, wa):
        exchanged(z, w)

    loads[-2].wait()
    loads[-1].wait()
    for copy in q_copies:
        copy.wait_recv()
    q_sum = q_part[0]
    for o in range(1, wa):
        q_sum = q_sum + q_in[o]
    q_sum = q_sum.astype(jnp.bfloat16)
    for h in range(heads):
        qs[:, pl.ds(h * rows, rows)] = jnp.transpose(q_sum[:, h * hd : (h + 1) * hd])
        gs[:, pl.ds(h * rows, rows)] = jnp.transpose(grad[:, h * hd : (h + 1) * hd])

    group_rows = rows // 128
    first_look = (z * ka + c) * group_rows
    look = jnp.concatenate(
        [look_ref[pl.ds(first_look + i, 1), :] for i in range(group_rows)] * heads, axis=1
    )
    last_key = (z * ka + c) * rows + jnp.concatenate(
        [lax.broadcasted_iota(jnp.int32, (1, rows), 1)] * heads, axis=1
    )
    before_key = last_key - look

    def products(t):
        key_pos = t * piece + lax.broadcasted_iota(jnp.int32, (piece, lanes), 0)
        visible = (key_pos <= last_key) & (key_pos > before_key)
        both = dot(
            jnp.concatenate([side[t, :, pl.ds(0, hd)], side[t, :, pl.ds(2 * hd, hd)]], axis=0),
            qs[...],
        )
        scores = both[:piece] * scale
        patched = both[piece:] * scale
        grad_value = dot(side[t, :, pl.ds(hd, hd)], gs[...])
        return (
            jnp.where(visible, scores, very_low),
            jnp.where(visible, patched, very_low),
            grad_value,
        )

    top[...] = jnp.full((1, lanes), very_low, jnp.float32)
    total[...] = jnp.zeros((1, lanes), jnp.float32)
    weighted[...] = jnp.zeros((1, lanes), jnp.float32)

    def stats(pieces):
        parts = []
        highest = top[...]
        for t in pieces:
            scores, patched, grad_value = products(t)
            if keep:
                kept[t, 0] = scores
                kept[t, 1] = patched
                kept[t, 2] = grad_value
            parts.append((scores, grad_value))
            highest = jnp.maximum(highest, jnp.max(scores, axis=0, keepdims=True))
        rescale = jnp.exp2(top[...] - highest)
        sums = total[...] * rescale
        products_sum = weighted[...] * rescale
        for scores, grad_value in parts:
            weights = jnp.exp2(scores - highest)
            sums = sums + jnp.sum(weights, axis=0, keepdims=True)
            products_sum = products_sum + jnp.sum(weights * grad_value, axis=0, keepdims=True)
        total[...] = sums
        weighted[...] = products_sum
        top[...] = highest

    def lanes_of(zz, cc):
        return [owner(zz, cc, xx) for xx in range(wa)]

    def other_core(zz, o):
        cc = lax.rem(c + ka - o, ka)
        for w in range(wa):
            block = side.at[owner(zz, cc, peer(wa - w))]
            remote(
                block, block, sib_send.at[zz, w, o], sib_recv.at[zz, w, ka - o], {"ka": cc}
            ).wait_recv()

    stats(lanes_of(z, c))
    for o in range(1, ka):

        @pl.when(c >= o)
        def _():
            other_core(z, o)
            stats(lanes_of(z, lax.rem(c + ka - o, ka)))

    def group(s, carry):
        @pl.when(s <= z)
        def _():
            zz = z - s

            @pl.when(s < z)
            def _():
                arrive(zz - 1)

            for w in range(1, wa):
                exchanged(zz, w)
            for o in range(1, ka):
                other_core(zz, o)
            stats([t for cc in range(ka) for t in lanes_of(zz, cc)])

        return carry

    lax.fori_loop(1, pb, group, 0)

    mean[...] = weighted[...] * pl.reciprocal(
        jnp.maximum(total[...], 1.0), full_range=False
    )

    step = 32

    def att_copy(t):
        return remote(att.at[t], att_in.at[me], att_send.at[t], att_recv.at[me], place(t))

    def piece_changes(t, slot):
        kt = t if keep else slot
        if not keep:
            scores, patched, grad_value = products(t)
            kept[kt, 0] = scores
            kept[kt, 1] = patched
            kept[kt, 2] = grad_value
        columns = []
        for k in range(piece // step):
            keys = pl.ds(k * step, step)
            so_far = jnp.zeros((step, 128), jnp.float32)
            for q in range(lanes // 128):
                cols = pl.ds(q * 128, 128)
                high = top[:, cols]
                away = kept[kt, 1, keys, cols] - high
                small = jnp.exp2(-jnp.abs(away))
                above = away > 0.0
                factor = jnp.where(above, small, 1.0)
                swapped = (
                    jnp.where(above, 1.0, small)
                    - jnp.exp2(kept[kt, 0, keys, cols] - high) * factor
                )
                divisor = jnp.maximum(total[:, cols] * factor + swapped, 1.0)
                upper = weighted[:, cols] * factor + swapped * kept[kt, 2, keys, cols]
                inverse = pl.reciprocal(divisor, full_range=False)
                so_far = so_far + (upper * inverse - mean[:, cols])
            columns.append(so_far)
        summed = jnp.concatenate(columns, axis=0)
        return jnp.sum(jnp.transpose(summed), axis=0, keepdims=True)

    def changes(b, carry):
        @pl.when(b <= z * ka + c)
        def _():
            result = [piece_changes(b * wa + p, p) for p in range(wa)]
            for p in range(wa):
                att[b * wa + p] = result[p]
            for p in range(wa):

                @pl.when(b * wa + p != me)
                def _():
                    att_copy(b * wa + p).start()

        return carry

    lax.fori_loop(0, pb * ka, changes, 0)

    out_ref[...] = att[me]

    def collect(t, carry):
        @pl.when((t != me) & (t // wa >= z * ka + c))
        def _():
            remote(
                att.at[t], att_in.at[t], att_send.at[t], att_recv.at[t], place(t)
            ).wait_recv()
            out_ref[...] += att_in[t]

        return carry

    lax.fori_loop(0, members, collect, 0)

    for copy in kv_copies + nk_copies + q_copies:
        copy.wait_send()

    def drain(zz, carry):
        @pl.when(zz <= z)
        def _():
            @pl.when(z + 1 < pb)
            def _():
                up(zz).wait_send()

            @pl.when(goes_along(zz))
            def _():
                for o in range(1, wa):
                    along(zz, o).wait_send()

            @pl.when(goes_up(zz))
            def _():
                for w in range(1, wa):
                    next_up(zz, w).wait_send()

            for w in range(wa):
                for o in range(1, ka):

                    @pl.when((zz < z) | (c + o < ka))
                    def _():
                        across(zz, w, o).wait_send()

        return carry

    lax.fori_loop(0, pb, drain, 0)

    def drain_att(t, carry):
        @pl.when((t != me) & (t // wa <= z * ka + c))
        def _():
            att_copy(t).wait_send()

        return carry

    lax.fori_loop(0, members, drain_att, 0)


def shards(clean_rows, noised_rows, query_weight, key_weight, value_weight, out_grads, lookback):
    pb, ka, wa = lax.axis_size("pb"), lax.axis_size("ka"), lax.axis_size("wa")
    rows, depth = clean_rows.shape
    hd = key_weight.shape[1]
    head_cols = out_grads.shape[1]
    heads = head_cols // hd
    lanes = heads * rows
    piece = rows // wa
    members = pb * ka * wa
    keep = members * 3 * piece * lanes * 4 <= keep_limit
    kept_shape = (members if keep else wa, 3, piece, lanes)
    sizes = (pb, ka, wa, rows, hd, heads, keep)
    bf16, f32 = jnp.bfloat16, jnp.float32
    vmem = pltpu.VMEM
    sem = pltpu.SemaphoreType.DMA
    out = pl.pallas_call(
        functools.partial(kernel, sizes),
        out_shape=jax.ShapeDtypeStruct((1, piece), f32),
        in_specs=[pl.BlockSpec(memory_space=pl.ANY)] * 7,
        out_specs=pl.BlockSpec(memory_space=vmem),
        scratch_shapes=[
            vmem((rows, depth), bf16),
            vmem((rows, depth), bf16),
            vmem((wa, depth, head_cols), bf16),
            vmem((depth, 2 * hd), bf16),
            vmem((rows, head_cols), bf16),
            vmem((rows, 2 * hd), f32),
            vmem((rows, hd), f32),
            vmem((wa, rows, head_cols), f32),
            vmem((wa, piece, 2 * hd), f32),
            vmem((wa, piece, hd), f32),
            vmem((wa, rows, head_cols), f32),
            vmem((members, piece, 3 * hd), bf16),
            vmem((hd, lanes), bf16),
            vmem((hd, lanes), bf16),
            vmem(kept_shape, f32),
            vmem((1, lanes), f32),
            vmem((1, lanes), f32),
            vmem((1, lanes), f32),
            vmem((1, lanes), f32),
            vmem((members, 1, piece), f32),
            vmem((members, 1, piece), f32),
            vmem((members * piece // 128, 128), jnp.int32),
            sem((11 + wa,)),
            sem((wa,)),
            sem((wa,)),
            sem((wa,)),
            sem((wa,)),
            sem((wa,)),
            sem((wa,)),
            sem((pb, wa)),
            sem((pb, wa)),
            sem((pb,)),
            sem((pb,)),
            sem((pb, wa)),
            sem((pb, wa)),
            sem((pb, wa, ka)),
            sem((pb, wa, ka)),
            sem((members,)),
            sem((members,)),
        ],
        compiler_params=pltpu.CompilerParams(
            collective_id=0, has_side_effects=True, vmem_limit_bytes=vmem_limit
        ),
    )(
        clean_rows,
        noised_rows,
        query_weight,
        key_weight,
        value_weight,
        out_grads,
        lookback.reshape(-1, 128),
    )
    return out.reshape(piece)


def solution(mesh):
    in_specs = (
        P(("pairs", "pb", "ka"), "wa"),
        P(("pairs", "pb", "ka"), "wa"),
        P("wa", None),
        P("wa", None),
        P("wa", None),
        P(("pairs", "pb", "ka"), "wa"),
        P("pairs"),
    )
    out_specs = P(("pairs", "pb", "ka", "wa"))
    return jax.shard_map(shards, mesh=mesh, in_specs=in_specs, out_specs=out_specs, check_vma=False)
```

```python
import functools
import math

import jax
import jax.numpy as jnp
from jax import lax
from jax.experimental import pallas as pl
from jax.experimental.pallas import tpu as pltpu
from jax.sharding import PartitionSpec as P

very_low = -1e30
keep_limit = 24 * 2**20
vmem_limit = 56 * 2**20
reach = 2
MESH = pl.DeviceIdType.MESH


def dot(left, right):
    return jnp.dot(left, right, preferred_element_type=jnp.float32)


def kernel(
    sizes,
    clean_hbm,
    noised_hbm,
    wq_hbm,
    wk_hbm,
    wv_hbm,
    grad_hbm,
    look_hbm,
    out_ref,
    clean,
    noised,
    wq,
    wkv,
    grad,
    kv_part,
    nk_part,
    q_part,
    kv_in,
    nk_in,
    q_in,
    side,
    qs,
    gs,
    kept,
    top,
    total,
    weighted,
    mean,
    att,
    att_in,
    look_ref,
    load_sem,
    kv_send,
    kv_recv,
    nk_send,
    nk_recv,
    q_send,
    q_recv,
    ag_send,
    ag_recv,
    z_send,
    z_recv,
    next_send,
    next_recv,
    sib_send,
    sib_recv,
    att_send,
    att_recv,
):
    pb, ka, wa, rows, hd, heads, keep = sizes
    piece = rows // wa
    head_cols = heads * hd
    lanes = heads * rows
    scale = math.log2(math.e) / math.sqrt(hd)
    members = pb * ka * wa
    z = lax.axis_index("pb")
    c = lax.axis_index("ka")
    x = lax.axis_index("wa")
    me = (z * ka + c) * wa + x

    def peer(o):
        return lax.rem(x + o, wa)

    half = clean.shape[1] // 2
    loads = []
    for i in range(2):
        part = pl.ds(i * half, half)
        loads += [
            pltpu.make_async_copy(
                clean_hbm.at[:, part], clean.at[:, part], load_sem.at[5 + wa + 3 * i]
            ),
            pltpu.make_async_copy(
                wk_hbm.at[part], wkv.at[part, pl.ds(0, hd)], load_sem.at[6 + wa + 3 * i]
            ),
            pltpu.make_async_copy(
                wv_hbm.at[part], wkv.at[part, pl.ds(hd, hd)], load_sem.at[7 + wa + 3 * i]
            ),
        ]
    loads.append(pltpu.make_async_copy(noised_hbm, noised, load_sem.at[3]))
    orders = list(range(1, wa)) + [0]
    for o in orders:
        cols = pl.ds(pl.multiple_of(peer(o) * head_cols, 128), head_cols)
        loads.append(pltpu.make_async_copy(wq_hbm.at[:, cols], wq.at[o], load_sem.at[5 + o]))
    loads.append(pltpu.make_async_copy(grad_hbm, grad, load_sem.at[4]))
    loads.append(pltpu.make_async_copy(look_hbm, look_ref, load_sem.at[0]))
    for load in loads:
        load.start()

    barrier = pltpu.get_barrier_semaphore()

    def place(t):
        return {"pb": t // (ka * wa), "ka": (t // wa) % ka, "wa": t % wa}

    def greet(t, carry):
        @pl.when(t != me)
        def _():
            pl.semaphore_signal(barrier, inc=1, device_id=place(t), device_id_type=MESH)

        return carry

    lax.fori_loop(0, members, greet, 0)

    def remote(src, dst, send, recv, where):
        return pltpu.make_async_remote_copy(
            src_ref=src,
            dst_ref=dst,
            send_sem=send,
            recv_sem=recv,
            device_id=where,
            device_id_type=MESH,
        )

    def part_rows(p):
        return pl.ds(pl.multiple_of(p * piece, piece), piece)

    for load in loads[:3]:
        load.wait()
    kv_part[...] = dot(clean[:, :half], wkv[:half, :])
    for load in loads[3:6]:
        load.wait()
    kv_part[...] += dot(clean[:, half:], wkv[half:, :])
    pl.semaphore_wait(barrier, members - 1)
    kv_copies = []
    for o in range(1, wa):
        p = peer(o)
        copy = remote(
            kv_part.at[part_rows(p)], kv_in.at[wa - o], kv_send.at[o], kv_recv.at[wa - o], {"wa": p}
        )
        copy.start()
        kv_copies.append(copy)
    loads[6].wait()
    nk_part[...] = dot(noised[...], wkv[:, :hd])
    nk_copies = []
    for o in range(1, wa):
        p = peer(o)
        copy = remote(
            nk_part.at[part_rows(p)], nk_in.at[wa - o], nk_send.at[o], nk_recv.at[wa - o], {"wa": p}
        )
        copy.start()
        nk_copies.append(copy)
    q_copies = []
    for n, o in enumerate(orders[:-1]):
        loads[7 + n].wait()
        q_part[o] = dot(clean[...], wq[o])
        copy = remote(
            q_part.at[o], q_in.at[wa - o], q_send.at[o], q_recv.at[wa - o], {"wa": peer(o)}
        )
        copy.start()
        q_copies.append(copy)

    mine = part_rows(x)
    for copy in kv_copies:
        copy.wait_recv()
    kv_sum = kv_part[mine, :]
    for o in range(1, wa):
        kv_sum = kv_sum + kv_in[o]
    side[me, :, pl.ds(0, 2 * hd)] = kv_sum.astype(jnp.bfloat16)
    for copy in nk_copies:
        copy.wait_recv()
    nk_sum = nk_part[mine, :]
    for o in range(1, wa):
        nk_sum = nk_sum + nk_in[o]
    side[me, :, pl.ds(2 * hd, hd)] = nk_sum.astype(jnp.bfloat16)

    def owner(zz, cc, xx):
        return (zz * ka + cc) * wa + xx

    def up(zz):
        block = side.at[owner(zz, c, x)]
        return remote(block, block, z_send.at[zz], z_recv.at[zz], {"pb": z + 1})

    def along(zz, o):
        block = side.at[owner(zz, c, x)]
        return remote(block, block, ag_send.at[zz, o], ag_recv.at[zz, wa - o], {"wa": peer(o)})

    def across(zz, w, o):
        block = side.at[owner(zz, c, peer(wa - w))]
        return remote(
            block,
            block,
            sib_send.at[zz, w, o],
            sib_recv.at[zz, w, ka - o],
            {"ka": lax.rem(c + o, ka)},
        )

    def next_up(zz, w):
        block = side.at[owner(zz, c, peer(wa - w))]
        return remote(block, block, next_send.at[zz, w], next_recv.at[zz, w], {"pb": z + 1})

    def goes_up(zz):
        return (z + 1 < pb) & (z + 1 - zz <= reach)

    def goes_along(zz):
        return (zz == z) | (z - zz > reach)

    def hand_over(zz, w):
        for o in range(1, ka):

            @pl.when((zz < z) | (c + o < ka))
            def _():
                across(zz, w, o).start()

    def pass_on(zz):
        @pl.when(z + 1 < pb)
        def _():
            up(zz).start()

        @pl.when(goes_along(zz))
        def _():
            for o in range(1, wa):
                along(zz, o).start()

        hand_over(zz, 0)

    def exchanged(zz, w):
        block = side.at[owner(zz, c, peer(wa - w))]

        @pl.when(goes_along(zz))
        def _():
            remote(
                block, block, ag_send.at[zz, w], ag_recv.at[zz, wa - w], {"wa": peer(w)}
            ).wait_recv()

        @pl.when(~goes_along(zz))
        def _():
            remote(
                block, block, next_send.at[zz, w], next_recv.at[zz, w], {"pb": z - 1}
            ).wait_recv()

        @pl.when(goes_up(zz))
        def _():
            next_up(zz, w).start()

        hand_over(zz, w)

    def arrive(zz):
        block = side.at[owner(zz, c, x)]
        remote(block, block, z_send.at[zz], z_recv.at[zz], {"pb": z - 1}).wait_recv()
        pass_on(zz)

    pass_on(z)
    loads[6 + wa].wait()
    q_part[0] = dot(clean[...], wq[0])

    @pl.when(z >= 1)
    def _():
        arrive(z - 1)

    @pl.when(z >= 2)
    def _():
        arrive(z - 2)

    for w in range(1, wa):
        exchanged(z, w)

    loads[-2].wait()
    loads[-1].wait()
    for copy in q_copies:
        copy.wait_recv()
    q_sum = q_part[0]
    for o in range(1, wa):
        q_sum = q_sum + q_in[o]
    q_sum = q_sum.astype(jnp.bfloat16)
    for h in range(heads):
        qs[:, pl.ds(h * rows, rows)] = jnp.transpose(q_sum[:, h * hd : (h + 1) * hd])
        gs[:, pl.ds(h * rows, rows)] = jnp.transpose(grad[:, h * hd : (h + 1) * hd])

    group_rows = rows // 128
    first_look = (z * ka + c) * group_rows
    look = jnp.concatenate(
        [look_ref[pl.ds(first_look + i, 1), :] for i in range(group_rows)] * heads, axis=1
    )
    last_key = (z * ka + c) * rows + jnp.concatenate(
        [lax.broadcasted_iota(jnp.int32, (1, rows), 1)] * heads, axis=1
    )
    before_key = last_key - look

    def products(t):
        key_pos = t * piece + lax.broadcasted_iota(jnp.int32, (piece, lanes), 0)
        visible = (key_pos <= last_key) & (key_pos > before_key)
        both = dot(
            jnp.concatenate([side[t, :, pl.ds(0, hd)], side[t, :, pl.ds(2 * hd, hd)]], axis=0),
            qs[...],
        )
        scores = both[:piece] * scale
        patched = both[piece:] * scale
        grad_value = dot(side[t, :, pl.ds(hd, hd)], gs[...])
        return (
            jnp.where(visible, scores, very_low),
            jnp.where(visible, patched, very_low),
            grad_value,
        )

    top[...] = jnp.full((1, lanes), very_low, jnp.float32)
    total[...] = jnp.zeros((1, lanes), jnp.float32)
    weighted[...] = jnp.zeros((1, lanes), jnp.float32)

    def stats(pieces):
        parts = []
        highest = top[...]
        for t in pieces:
            scores, patched, grad_value = products(t)
            if keep:
                kept[t, 0] = scores
                kept[t, 1] = patched
                kept[t, 2] = grad_value
            parts.append((scores, grad_value))
            highest = jnp.maximum(highest, jnp.max(scores, axis=0, keepdims=True))
        rescale = jnp.exp2(top[...] - highest)
        sums = total[...] * rescale
        products_sum = weighted[...] * rescale
        for scores, grad_value in parts:
            weights = jnp.exp2(scores - highest)
            sums = sums + jnp.sum(weights, axis=0, keepdims=True)
            products_sum = products_sum + jnp.sum(weights * grad_value, axis=0, keepdims=True)
        total[...] = sums
        weighted[...] = products_sum
        top[...] = highest

    def lanes_of(zz, cc):
        return [owner(zz, cc, xx) for xx in range(wa)]

    def other_core(zz, o):
        cc = lax.rem(c + ka - o, ka)
        for w in range(wa):
            block = side.at[owner(zz, cc, peer(wa - w))]
            remote(
                block, block, sib_send.at[zz, w, o], sib_recv.at[zz, w, ka - o], {"ka": cc}
            ).wait_recv()

    stats(lanes_of(z, c))
    for o in range(1, ka):

        @pl.when(c >= o)
        def _():
            other_core(z, o)
            stats(lanes_of(z, lax.rem(c + ka - o, ka)))

    def group(s, carry):
        @pl.when(s <= z)
        def _():
            zz = z - s

            @pl.when(zz >= 2)
            def _():
                arrive(zz - 2)

            for w in range(1, wa):
                exchanged(zz, w)
            for o in range(1, ka):
                other_core(zz, o)
            stats([t for cc in range(ka) for t in lanes_of(zz, cc)])

        return carry

    lax.fori_loop(1, pb, group, 0)

    mean[...] = weighted[...] * pl.reciprocal(
        jnp.maximum(total[...], 1.0), full_range=False
    )

    step = 32

    def att_copy(t):
        return remote(att.at[t], att_in.at[me], att_send.at[t], att_recv.at[me], place(t))

    def piece_changes(t, slot):
        kt = t if keep else slot
        if not keep:
            scores, patched, grad_value = products(t)
            kept[kt, 0] = scores
            kept[kt, 1] = patched
            kept[kt, 2] = grad_value
        columns = []
        for k in range(piece // step):
            keys = pl.ds(k * step, step)
            so_far = jnp.zeros((step, 128), jnp.float32)
            for q in range(lanes // 128):
                cols = pl.ds(q * 128, 128)
                high = top[:, cols]
                away = kept[kt, 1, keys, cols] - high
                small = jnp.exp2(-jnp.abs(away))
                above = away > 0.0
                factor = jnp.where(above, small, 1.0)
                swapped = (
                    jnp.where(above, 1.0, small)
                    - jnp.exp2(kept[kt, 0, keys, cols] - high) * factor
                )
                divisor = jnp.maximum(total[:, cols] * factor + swapped, 1.0)
                upper = weighted[:, cols] * factor + swapped * kept[kt, 2, keys, cols]
                inverse = pl.reciprocal(divisor, full_range=False)
                so_far = so_far + (upper * inverse - mean[:, cols])
            columns.append(so_far)
        summed = jnp.concatenate(columns, axis=0)
        return jnp.sum(jnp.transpose(summed), axis=0, keepdims=True)

    def changes(b, carry):
        @pl.when(b <= z * ka + c)
        def _():
            result = [piece_changes(b * wa + p, p) for p in range(wa)]
            for p in range(wa):
                att[b * wa + p] = result[p]
            for p in range(wa):

                @pl.when(b * wa + p != me)
                def _():
                    att_copy(b * wa + p).start()

        return carry

    lax.fori_loop(0, pb * ka, changes, 0)

    out_ref[...] = att[me]

    def collect(t, carry):
        @pl.when((t != me) & (t // wa >= z * ka + c))
        def _():
            remote(
                att.at[t], att_in.at[t], att_send.at[t], att_recv.at[t], place(t)
            ).wait_recv()
            out_ref[...] += att_in[t]

        return carry

    lax.fori_loop(0, members, collect, 0)

    for copy in kv_copies + nk_copies + q_copies:
        copy.wait_send()

    def drain(zz, carry):
        @pl.when(zz <= z)
        def _():
            @pl.when(z + 1 < pb)
            def _():
                up(zz).wait_send()

            @pl.when(goes_along(zz))
            def _():
                for o in range(1, wa):
                    along(zz, o).wait_send()

            @pl.when(goes_up(zz))
            def _():
                for w in range(1, wa):
                    next_up(zz, w).wait_send()

            for w in range(wa):
                for o in range(1, ka):

                    @pl.when((zz < z) | (c + o < ka))
                    def _():
                        across(zz, w, o).wait_send()

        return carry

    lax.fori_loop(0, pb, drain, 0)

    def drain_att(t, carry):
        @pl.when((t != me) & (t // wa <= z * ka + c))
        def _():
            att_copy(t).wait_send()

        return carry

    lax.fori_loop(0, members, drain_att, 0)


def shards(clean_rows, noised_rows, query_weight, key_weight, value_weight, out_grads, lookback):
    pb, ka, wa = lax.axis_size("pb"), lax.axis_size("ka"), lax.axis_size("wa")
    rows, depth = clean_rows.shape
    hd = key_weight.shape[1]
    head_cols = out_grads.shape[1]
    heads = head_cols // hd
    lanes = heads * rows
    piece = rows // wa
    members = pb * ka * wa
    keep = members * 3 * piece * lanes * 4 <= keep_limit
    kept_shape = (members if keep else wa, 3, piece, lanes)
    sizes = (pb, ka, wa, rows, hd, heads, keep)
    bf16, f32 = jnp.bfloat16, jnp.float32
    vmem = pltpu.VMEM
    sem = pltpu.SemaphoreType.DMA
    out = pl.pallas_call(
        functools.partial(kernel, sizes),
        out_shape=jax.ShapeDtypeStruct((1, piece), f32),
        in_specs=[pl.BlockSpec(memory_space=pl.ANY)] * 7,
        out_specs=pl.BlockSpec(memory_space=vmem),
        scratch_shapes=[
            vmem((rows, depth), bf16),
            vmem((rows, depth), bf16),
            vmem((wa, depth, head_cols), bf16),
            vmem((depth, 2 * hd), bf16),
            vmem((rows, head_cols), bf16),
            vmem((rows, 2 * hd), f32),
            vmem((rows, hd), f32),
            vmem((wa, rows, head_cols), f32),
            vmem((wa, piece, 2 * hd), f32),
            vmem((wa, piece, hd), f32),
            vmem((wa, rows, head_cols), f32),
            vmem((members, piece, 3 * hd), bf16),
            vmem((hd, lanes), bf16),
            vmem((hd, lanes), bf16),
            vmem(kept_shape, f32),
            vmem((1, lanes), f32),
            vmem((1, lanes), f32),
            vmem((1, lanes), f32),
            vmem((1, lanes), f32),
            vmem((members, 1, piece), f32),
            vmem((members, 1, piece), f32),
            vmem((members * piece // 128, 128), jnp.int32),
            sem((11 + wa,)),
            sem((wa,)),
            sem((wa,)),
            sem((wa,)),
            sem((wa,)),
            sem((wa,)),
            sem((wa,)),
            sem((pb, wa)),
            sem((pb, wa)),
            sem((pb,)),
            sem((pb,)),
            sem((pb, wa)),
            sem((pb, wa)),
            sem((pb, wa, ka)),
            sem((pb, wa, ka)),
            sem((members,)),
            sem((members,)),
        ],
        compiler_params=pltpu.CompilerParams(
            collective_id=0, has_side_effects=True, vmem_limit_bytes=vmem_limit
        ),
    )(
        clean_rows,
        noised_rows,
        query_weight,
        key_weight,
        value_weight,
        out_grads,
        lookback.reshape(-1, 128),
    )
    return out.reshape(piece)


def solution(mesh):
    in_specs = (
        P(("pairs", "pb", "ka"), "wa"),
        P(("pairs", "pb", "ka"), "wa"),
        P("wa", None),
        P("wa", None),
        P("wa", None),
        P(("pairs", "pb", "ka"), "wa"),
        P("pairs"),
    )
    out_specs = P(("pairs", "pb", "ka", "wa"))
    return jax.shard_map(shards, mesh=mesh, in_specs=in_specs, out_specs=out_specs, check_vma=False)
```
